256 devices in a mesh: leaf: 32 (over z_lo, x, core), seq: 8 (over z_hi, y).
Axes of the slice: x: 4, y: 4, z: 8 (z_hi: 2, z_lo: 4; z = z_hi * 4 + z_lo), core: 2. Of those that a mesh axis runs over, the one named last changes fastest.
Arguments:
- latents: bfloat16 [32, 16, 128, 1024], P('leaf', 'seq'), may hold values from -6 to 6
- keyframes: bfloat16 [32, 128, 1024], P('leaf', 'seq'), may hold values from -6 to 6
- key_index: int32 [32, 2], P('leaf'), may hold values from 0 to 31
- timesteps: int32 [2], replicated, may hold values from 0 to 999
- mod_weight: bfloat16 [256, 2048], replicated, may hold values from -0.375 to 0.375
- norm_gain: float32 [1024], replicated, may hold values from 0.5 to 1.5
- qkv_weight: bfloat16 [1024, 3072], replicated, may hold values from -0.1875 to 0.1875
- query_gain: float32 [64], replicated, may hold values from 1 to 2
- key_gain: float32 [64], replicated, may hold values from 1 to 2
- out_weight: bfloat16 [1024, 1024], replicated, may hold values from -0.75 to 0.75
Outputs:
- denoised: bfloat16 [32, 16, 128, 1024], P('leaf', 'seq')
The draws below stay inside these ranges and needn't reach their ends.
All inputs are finite; a program needn't handle non-finite values.
Results may differ from the reference program's by a relative error of at most 0.009.
Values may be sent and summed in bfloat16 or wider, within the bound.
No kernel may reach another device: no remote copies, remote signals or barrier semaphores. Data moves between devices by JAX's collectives and lax.ppermute only.
A program may use at most 128 MiB of HBM per device.

```python
import math
import jax
import jax.numpy as jnp
from jax import lax

HEADS = 16
HEAD = 64
TEMB = 256
TSTEPS = 1000
TOKF = 128
D = 1024
CLIPS = 32
FRAMES = 16
KEYS = 32


def set_ends(entries, stream_key, least, high):
    place = [jax.random.randint(jax.random.fold_in(stream_key, axis), (), 0, length) for axis, length in enumerate(entries.shape)]
    longest = entries.shape.index(max(entries.shape))
    next_to = place[:longest] + [(place[longest] + 1) % entries.shape[longest]] + place[longest + 1:]
    return entries.at[tuple(place)].set(least).at[tuple(next_to)].set(high)


def block_levels(rng, extent, split, smallest, top_value):
    level, own = 1.0, jax.random.fold_in(rng, 6)
    for position, parts in split:
        heights = jnp.exp(jax.random.uniform(jax.random.fold_in(own, position), (parts,), jnp.float32, smallest / len(split), top_value / len(split)))
        level = level * jnp.repeat(heights, extent[position] // parts).reshape([-1 if axis == position else 1 for axis in range(len(extent))])
    return level


def normal_values(key, extent, spread, reach, pieces=(), held_as=jnp.bfloat16):
    result = jax.random.normal(key, extent, jnp.float32) * spread
    if len(pieces) > 0:
        result = block_levels(key, extent, pieces, -0.22, 0.18) * result
    return jnp.clip(result, min=-reach, max=reach).astype(held_as)


def setup_inputs(seed: int = 0) -> dict:
    arg_keys = jax.random.split(jax.random.key(seed), 11)
    latents = normal_values(arg_keys[0], (CLIPS, FRAMES, TOKF, D), 1.0, 6.0, ((0, 32), (1, 8)))
    keyframes = normal_values(arg_keys[1], (KEYS, TOKF, D), 1.0, 6.0, ((0, 32), (1, 8)))
    key_index = set_ends(jax.random.randint(arg_keys[2], (CLIPS, 2), 0, KEYS), jax.random.fold_in(arg_keys[2], 1), 0, KEYS - 1).astype(jnp.int32)
    timesteps = jax.random.randint(arg_keys[3], (2,), 0, TSTEPS).astype(jnp.int32)
    mod_weight = normal_values(arg_keys[4], (TEMB, 2 * D), TEMB ** -0.5, 0.375)
    norm_gain = jnp.clip(1.0 + 0.1 * jax.random.normal(arg_keys[5], (D,), jnp.float32), 0.5, 1.5)
    qkv_weight = normal_values(arg_keys[6], (D, 3 * D), D ** -0.5, 0.1875)
    query_gain = jnp.clip(jnp.exp(jax.random.uniform(arg_keys[7], (HEAD,), jnp.float32, math.log(1.0), math.log(2.0))), 1.0, 2.0)
    key_gain = jnp.clip(jnp.exp(jax.random.uniform(arg_keys[8], (HEAD,), jnp.float32, math.log(1.0), math.log(2.0))), 1.0, 2.0)
    out_weight = normal_values(arg_keys[9], (D, D), (D // 16) ** -0.5, 0.75)
    return dict(latents=latents, keyframes=keyframes, key_index=key_index, timesteps=timesteps, mod_weight=mod_weight, norm_gain=norm_gain, qkv_weight=qkv_weight, query_gain=query_gain, key_gain=key_gain, out_weight=out_weight)


def head_norm(values, gain):
    return values * lax.rsqrt(lax.optimization_barrier(jnp.mean(values * values, axis=-1, keepdims=True)) + 1e-06) * gain

def reference(latents, keyframes, key_index, timesteps, mod_weight, norm_gain, qkv_weight, query_gain, key_gain, out_weight):
    halfway = TEMB // 2
    freqs = jnp.exp(-math.log(10000.0) * jnp.arange(halfway, dtype=jnp.float32) / halfway)
    angles = timesteps[1].astype(jnp.float32) * freqs
    embed = jnp.concatenate([jnp.sin(angles), jnp.cos(angles)]).astype(jnp.bfloat16)
    modulation = jnp.dot(embed[None, :], mod_weight, preferred_element_type=jnp.float32)[0]
    scale = modulation[:D]
    shift = modulation[D:]
    key_weight = 1.0 - timesteps[0].astype(jnp.float32) / (2.0 * TSTEPS)
    ramp = jnp.arange(FRAMES, dtype=jnp.float32) / max(FRAMES - 1, 1)
    count = FRAMES * TOKF

    def one_clip(inputs):
        clip, pair = inputs
        first = keyframes[pair[0]].astype(jnp.float32)
        last = keyframes[pair[1]].astype(jnp.float32)
        blend = (1.0 - ramp)[:, None, None] * first[None] + ramp[:, None, None] * last[None]
        resid = (clip.astype(jnp.float32) + key_weight * blend).reshape(count, D)
        mean = lax.optimization_barrier(jnp.mean(resid, axis=-1, keepdims=True))
        var = lax.optimization_barrier(jnp.mean((resid - mean) ** 2, axis=-1, keepdims=True))
        normed = ((resid - mean) * lax.rsqrt(var + 1e-06) * norm_gain * (1.0 + scale) + shift).astype(jnp.bfloat16)
        qkv = jnp.dot(normed, qkv_weight, preferred_element_type=jnp.float32).reshape(count, 3, HEADS, HEAD)
        queries = head_norm(qkv[:, 0], query_gain).astype(jnp.bfloat16).transpose(1, 0, 2)
        keys_all = head_norm(qkv[:, 1], key_gain).astype(jnp.bfloat16).transpose(1, 0, 2)
        values = qkv[:, 2].astype(jnp.bfloat16).transpose(1, 0, 2)

        def one_head(trio):
            query_h, key_h, value_h = trio
            scores = jnp.dot(query_h, key_h.T, preferred_element_type=jnp.float32) * HEAD ** (-0.5)
            weights = jnp.exp(scores)
            total = lax.optimization_barrier(jnp.sum(weights, axis=-1, keepdims=True))
            mixed = jnp.dot(weights.astype(jnp.bfloat16), value_h, preferred_element_type=jnp.float32)
            return (mixed / total).astype(jnp.bfloat16)
        attended = lax.map(one_head, (queries, keys_all, values)).transpose(1, 0, 2).reshape(count, D)
        output = resid + jnp.dot(attended, out_weight, preferred_element_type=jnp.float32)
        return output.astype(jnp.bfloat16).reshape(FRAMES, TOKF, D)
    return lax.map(one_clip, (latents, key_index))
```

```python
import functools
import math

import jax
import jax.numpy as jnp
from jax import lax
from jax.experimental import pallas as pl
from jax.experimental.pallas import tpu as pltpu
from jax.sharding import PartitionSpec as P

HEADS = 16
HEAD = 64
TEMB = 256
TSTEPS = 1000
D = 1024
FRAMES = 16
TOKF = 128
AXES = ("leaf", "seq")
ZL, X, CORE, ZH, Y = 4, 4, 2, 2, 4
ROWS = 256
PIECE = 16
PAIRS = HEADS // 2
F32 = jnp.float32
BF16 = jnp.bfloat16
QSCALE = HEAD ** (-0.5) * math.log2(math.e)


def moves(zl=0, x=0, core=0, zh=0, y=0):
    pairs = []
    for i in range(ZL * X * CORE * ZH * Y):
        rest, iy = divmod(i, Y)
        rest, izh = divmod(rest, ZH)
        rest, ic = divmod(rest, CORE)
        izl, ix = divmod(rest, X)
        izl, ix, ic = (izl + zl) % ZL, (ix + x) % X, (ic + core) % CORE
        izh, iy = (izh + zh) % ZH, (iy + y) % Y
        pairs.append((i, (((izl * X + ix) * CORE + ic) * ZH + izh) * Y + iy))
    return pairs


def send(value, **step):
    return lax.ppermute(value, AXES, moves(**step))


def dot(a, b):
    return jnp.dot(a, b, preferred_element_type=F32)


def dot_t(a, b):
    return lax.dot_general(a, b, (((1,), (1,)), ((), ())), preferred_element_type=F32)


def blend_tables(kw, piece_refs, base_ref, first_s, diff_s):
    for i, piece in enumerate(piece_refs):
        for z in range(ZH):
            base = pl.multiple_of(base_ref[i * ZH + z], PIECE)
            first = piece[z, 0].astype(F32) * kw
            last = piece[z, 1].astype(F32) * kw
            first_s[pl.ds(base, PIECE), :] = first
            diff_s[pl.ds(base, PIECE), :] = last - first


def norm_chunk(lat_ref, ramps, first_s, diff_s, gain_ref, shift_ref, x_s):
    step = 32

    def rows(i, carry):
        r = pl.multiple_of(i * step, step)
        tok = pl.multiple_of(lax.rem(i, TOKF // step) * step, step)
        ramp = jnp.where(i < TOKF // step, ramps[0], ramps[1])
        resid = lat_ref[pl.ds(r, step), :].astype(F32) + (
            first_s[pl.ds(tok, step), :] + ramp * diff_s[pl.ds(tok, step), :]
        )
        mean = jnp.mean(resid, axis=-1, keepdims=True)
        cent = resid - mean
        var = jnp.mean(cent * cent, axis=-1, keepdims=True)
        normed = cent * lax.rsqrt(var + 1e-06) * gain_ref[...] + shift_ref[...]
        x_s[pl.ds(r, step), :] = normed.astype(BF16)
        return carry

    lax.fori_loop(0, ROWS // step, rows, 0, unroll=2)


def head_norm_t(block, gain):
    heads = block.reshape(block.shape[0] // HEAD, HEAD, block.shape[1])
    mean = jnp.mean(heads * heads, axis=1, keepdims=True)
    return (heads * lax.rsqrt(mean + 1e-06) * gain[None]).reshape(block.shape)


def keys_values(j, x_s, wk_ref, wv_ref, kgain_ref, kt_s, v_s):
    def block(i, carry):
        f = pl.multiple_of(i * 256, 256)
        kt = dot_t(wk_ref[pl.ds(f, 256), :], x_s[...])
        kt_s[pl.ds(f, 256), j * ROWS : (j + 1) * ROWS] = head_norm_t(kt, kgain_ref[...]).astype(BF16)
        v = dot(x_s[...], wv_ref[:, pl.ds(f, 256)])
        v_s[j * ROWS : (j + 1) * ROWS, pl.ds(f, 256)] = v.astype(BF16)
        return carry

    lax.fori_loop(0, D // 256, block, 0)


def attend(q_ref, kt_s, v_s, acc_in, acc_out):
    lane_q = lax.broadcasted_iota(jnp.int32, (ROWS, 128), 1) < HEAD
    nkeys = kt_s.shape[1]
    lane_v = lax.broadcasted_iota(jnp.int32, (nkeys, 128), 1) < HEAD

    def pair(p, carry):
        f = pl.multiple_of(p * 128, 128)
        qp = q_ref[:, pl.ds(f, 128)]
        vp = v_s[:, pl.ds(f, 128)]
        one = jnp.ones((), BF16)
        zero = jnp.zeros((), BF16)
        for odd in range(2):
            keep = lane_q if odd == 0 else jnp.logical_not(lane_q)
            qh = jnp.where(keep, qp, zero)
            keepv = lane_v if odd == 0 else jnp.logical_not(lane_v)
            vh = jnp.where(keepv, vp, one)
            total = None
            for b in range(nkeys // 256):
                s = dot(qh, kt_s[pl.ds(f, 128), b * 256 : (b + 1) * 256])
                w = jnp.exp2(s).astype(BF16)
                o = dot(w, vh[b * 256 : (b + 1) * 256])
                total = o if total is None else total + o
            if acc_in is not None:
                total = total + acc_in[2 * p + odd]
            acc_out[2 * p + odd] = total
        return carry

    lax.fori_loop(0, PAIRS, pair, 0)


def first_kernel(
    fl_ref, base_ref, l0, l1, l2, l3, p0, p1, p2, p3, gain_ref, shift_ref, wq_ref, wk_ref, wv_ref,
    qgain_ref, kgain_ref, acc_ref, q_ref, first_s, diff_s, x_s, kt_s, v_s,
):
    blend_tables(fl_ref[0], (p0, p1, p2, p3), base_ref, first_s, diff_s)
    for j, lat in enumerate((l0, l1, l2, l3)):
        ramps = (fl_ref[1 + 2 * j], fl_ref[2 + 2 * j])
        norm_chunk(lat, ramps, first_s, diff_s, gain_ref, shift_ref, x_s)
        if j == 0:
            def block(i, carry):
                f = pl.multiple_of(i * 256, 256)
                qt = dot_t(wq_ref[pl.ds(f, 256), :], x_s[...])
                q = head_norm_t(qt, qgain_ref[...])
                q_ref[:, pl.ds(f, 256)] = q.T.astype(BF16)
                return carry

            lax.fori_loop(0, D // 256, block, 0)
        keys_values(j, x_s, wk_ref, wv_ref, kgain_ref, kt_s, v_s)
    attend(q_ref, kt_s, v_s, None, acc_ref)


def second_kernel(
    fl_ref, base_ref, own, l0, l1, l2, l3, p0, p1, p2, p3, gain_ref, shift_ref, wk_ref, wv_ref,
    kgain_ref, wo_ref, q_ref, acc_ref, out_ref, first_s, diff_s, x_s, kt_s, v_s, acc_s,
):
    blend_tables(fl_ref[0], (p0, p1, p2, p3), base_ref, first_s, diff_s)
    for j, lat in enumerate((l0, l1, l2, l3)):
        ramps = (fl_ref[1 + 2 * j], fl_ref[2 + 2 * j])
        norm_chunk(lat, ramps, first_s, diff_s, gain_ref, shift_ref, x_s)
        keys_values(j, x_s, wk_ref, wv_ref, kgain_ref, kt_s, v_s)
    attend(q_ref, kt_s, v_s, acc_ref, acc_s)

    lane = lax.broadcasted_iota(jnp.int32, (ROWS, 128), 1) < HEAD
    for p in range(PAIRS):
        even = acc_s[2 * p]
        odd = acc_s[2 * p + 1]
        num = jnp.where(lane, even, odd)
        den = pltpu.roll(jnp.where(lane, odd, even), HEAD, 1)
        x_s[:, p * 128 : (p + 1) * 128] = (num / den).astype(BF16)

    def block(i, carry):
        f = pl.multiple_of(i * 256, 256)
        o = dot(x_s[...], wo_ref[:, pl.ds(f, 256)])
        for k in range(2):
            r = slice(k * TOKF, (k + 1) * TOKF)
            resid = own[r, pl.ds(f, 256)].astype(F32) + (
                first_s[:, pl.ds(f, 256)] + fl_ref[9 + k] * diff_s[:, pl.ds(f, 256)]
            )
            out_ref[r, pl.ds(f, 256)] = (resid + o[r]).astype(BF16)
        return carry

    lax.fori_loop(0, D // 256, block, 0)


VMEM = pl.BlockSpec(memory_space=pltpu.VMEM)
SMEM = pl.BlockSpec(memory_space=pltpu.SMEM)


def scratch():
    return [
        pltpu.VMEM((TOKF, D), F32),
        pltpu.VMEM((TOKF, D), F32),
        pltpu.VMEM((ROWS, D), BF16),
        pltpu.VMEM((D, Y * ROWS), BF16),
        pltpu.VMEM((Y * ROWS, D), BF16),
    ]


def body(
    latents, keyframes, key_index, timesteps, mod_weight, norm_gain, qkv_weight, query_gain,
    key_gain, out_weight,
):
    place = lax.axis_index("leaf")
    seq = lax.axis_index("seq")
    zl, x, core = place // (X * CORE), place // CORE % X, place % CORE
    zh, y = seq // Y, seq % Y

    own = latents.reshape(ROWS, D)
    mine = keyframes[0]
    by_zl = [mine] + [send(mine, zl=k) for k in (1, 2, 3)]
    by_zl = jnp.stack(by_zl)
    near = [own] + [send(own, y=k) for k in (1, 2, 3)]
    by_x = jnp.stack([by_zl] + [send(by_zl, x=k) for k in (1, 2, 3)])
    by_core = jnp.stack([by_x, send(by_x, core=1)])
    pair = key_index[0]
    pick_zl = (zl - pair // (X * CORE)) % ZL
    pick_x = (x - pair // CORE % X) % X
    pick_c = (core + pair) % CORE
    pick = (pick_c * X + pick_x) * ZL + pick_zl
    flat = by_core.reshape(CORE * X * ZL, PIECE, D)
    chosen = jnp.stack([
        lax.dynamic_index_in_dim(flat, pick[0], 0, keepdims=False),
        lax.dynamic_index_in_dim(flat, pick[1], 0, keepdims=False),
    ])
    both = jnp.stack([chosen, send(chosen, zh=1)])
    pieces = [both] + [send(both, y=k) for k in (1, 2, 3)]
    cross = send(own, zh=1)
    far = [cross] + [send(cross, y=k) for k in (1, 2, 3)]

    halfway = TEMB // 2
    freqs = jnp.exp(-math.log(10000.0) * jnp.arange(halfway, dtype=F32) / halfway)
    angles = timesteps[1].astype(F32) * freqs
    embed = jnp.concatenate([jnp.sin(angles), jnp.cos(angles)]).astype(BF16)
    modulation = jnp.dot(embed[None, :], mod_weight, preferred_element_type=F32)
    gain = norm_gain[None, :] * (1.0 + modulation[:, :D])
    shift = modulation[:, D:]
    kw = 1.0 - timesteps[0].astype(F32) / (2.0 * TSTEPS)

    wq = qkv_weight[:, :D].T
    wk = qkv_weight[:, D : 2 * D].T
    wv = qkv_weight[:, 2 * D :]
    qgain = (query_gain * QSCALE)[:, None]
    kgain = key_gain[:, None]

    steps = jnp.arange(Y, dtype=jnp.int32)
    from_y = (y - steps) % Y
    two = jnp.arange(2, dtype=jnp.int32)

    def ramps(plane):
        frames = (plane * Y + from_y)[:, None] * 2 + two[None, :]
        return (frames.astype(F32) / (FRAMES - 1)).reshape(-1)

    planes = jnp.stack([zh, 1 - zh])
    base = ((planes[None, :] * Y + from_y[:, None]) * PIECE).reshape(-1).astype(jnp.int32)
    near_ramps, far_ramps = ramps(zh), ramps(1 - zh)
    fl_near = jnp.concatenate([kw[None], near_ramps])
    fl_far = jnp.concatenate([kw[None], far_ramps, near_ramps[:2]])

    flops = 2 * 1024 * 1024 * 2048 + 4 * 16 * 256 * 1024 * 128
    params = pltpu.CompilerParams(vmem_limit_bytes=48 * 1024 * 1024)
    acc, q = pl.pallas_call(
        first_kernel,
        out_shape=(
            jax.ShapeDtypeStruct((HEADS, ROWS, 128), F32),
            jax.ShapeDtypeStruct((ROWS, D), BF16),
        ),
        in_specs=[SMEM, SMEM] + [VMEM] * 15,
        out_specs=(VMEM, VMEM),
        scratch_shapes=scratch(),
        compiler_params=params,
        cost_estimate=pl.CostEstimate(flops=flops, bytes_accessed=12 << 20, transcendentals=4 << 20),
        name="near_keys",
    )(fl_near, base, *near, *pieces, gain, shift, wq, wk, wv, qgain, kgain)
    out = pl.pallas_call(
        second_kernel,
        out_shape=jax.ShapeDtypeStruct((ROWS, D), BF16),
        in_specs=[SMEM, SMEM] + [VMEM] * 17,
        out_specs=VMEM,
        scratch_shapes=scratch() + [pltpu.VMEM((HEADS, ROWS, 128), F32)],
        compiler_params=params,
        cost_estimate=pl.CostEstimate(flops=flops, bytes_accessed=12 << 20, transcendentals=4 << 20),
        name="far_keys",
    )(fl_far, base, own, *far, *pieces, gain, shift, wk, wv, kgain, out_weight, q, acc)
    return out.reshape(latents.shape)


def solution(mesh):
    in_specs = (
        P("leaf", "seq", None, None),
        P("leaf", "seq", None),
        P("leaf", None),
        P(),
        P(),
        P(),
        P(),
        P(),
        P(),
        P(),
    )
    out_specs = P("leaf", "seq", None, None)
    return jax.shard_map(body, mesh=mesh, in_specs=in_specs, out_specs=out_specs, check_vma=False)
```

```python
import math

import jax
import jax.numpy as jnp
import numpy as np
from jax import lax
from jax.experimental import pallas as pl
from jax.experimental.pallas import tpu as pltpu
from jax.sharding import Mesh
from jax.sharding import PartitionSpec as P

HEADS = 16
HEAD = 64
TEMB = 256
TSTEPS = 1000
D = 1024
FRAMES = 16
TOKF = 128
AXES = ("zl", "x", "core", "zh", "y")
ZL, X, CORE, ZH, Y = 4, 4, 2, 2, 4
ROWS = 256
PIECE = 16
PAIRS = HEADS // 2
F32 = jnp.float32
BF16 = jnp.bfloat16
QSCALE = HEAD ** (-0.5) * math.log2(math.e)


def moves(zl=0, x=0, core=0, zh=0, y=0):
    pairs = []
    for i in range(ZL * X * CORE * ZH * Y):
        rest, iy = divmod(i, Y)
        rest, izh = divmod(rest, ZH)
        rest, ic = divmod(rest, CORE)
        izl, ix = divmod(rest, X)
        izl, ix, ic = (izl + zl) % ZL, (ix + x) % X, (ic + core) % CORE
        izh, iy = (izh + zh) % ZH, (iy + y) % Y
        pairs.append((i, (((izl * X + ix) * CORE + ic) * ZH + izh) * Y + iy))
    return pairs


def send(value, **step):
    return lax.ppermute(value, AXES, moves(**step))


def after(value, earlier):
    return lax.optimization_barrier((value, earlier))[0]


def dot(a, b):
    return jnp.dot(a, b, preferred_element_type=F32)


def dot_tt(a, b):
    return lax.dot_general(a, b, (((0,), (1,)), ((), ())), preferred_element_type=F32)


def blend_tables(time_ref, pieces, base_ref, first_s, diff_s):
    kw = 1.0 - time_ref[0].astype(F32) * (1.0 / (2.0 * TSTEPS))
    for i, piece in enumerate(pieces):
        for z in range(ZH):
            base = pl.multiple_of(base_ref[ZH * i + z], PIECE)
            first = piece[0, z].astype(F32) * kw
            last = piece[1, z].astype(F32) * kw
            first_s[pl.ds(base, PIECE), :] = first
            diff_s[pl.ds(base, PIECE), :] = last - first


def norm_chunk(j, lat_ref, ramp_ref, at, first_s, diff_s, gain_ref, shift_ref, x_s):
    step = 32

    def rows(i, carry):
        r = pl.multiple_of(i * step, step)
        tok = pl.multiple_of(lax.rem(i, TOKF // step) * step, step)
        ramp = ramp_ref[at + i // (TOKF // step)]
        resid = lat_ref[pl.ds(r, step), :].astype(F32) + (
            first_s[pl.ds(tok, step), :] + ramp * diff_s[pl.ds(tok, step), :]
        )
        mean = jnp.mean(resid, axis=-1, keepdims=True)
        cent = resid - mean
        var = jnp.mean(cent * cent, axis=-1, keepdims=True)
        normed = cent * lax.rsqrt(var + 1e-06) * gain_ref[...] + shift_ref[...]
        x_s[pl.ds(pl.multiple_of(j * ROWS + i * step, step), step), :] = normed.astype(BF16)
        return carry

    lax.fori_loop(0, ROWS // step, rows, 0, unroll=4)


def head_norm_t(block, gain):
    heads = block.reshape(block.shape[0] // HEAD, HEAD, block.shape[1])
    mean = jnp.mean(heads * heads, axis=1, keepdims=True)
    return (heads * lax.rsqrt(mean + 1e-06) * gain[None]).reshape(block.shape)


def keys_values(x_s, w_ref, kgain_ref, kt_s, v_s):
    def values(i, carry):
        f = pl.multiple_of(i * 256, 256)
        v_s[:, pl.ds(f, 256)] = dot(x_s[...], w_ref[:, pl.ds(2 * D + f, 256)]).astype(BF16)
        return carry

    def keys(i, carry):
        t = pl.multiple_of(i * 256, 256)
        kt = dot_tt(w_ref[:, D : 2 * D], x_s[pl.ds(t, 256), :])
        kt_s[:, pl.ds(t, 256)] = head_norm_t(kt, kgain_ref[...]).astype(BF16)
        return carry

    lax.fori_loop(0, D // 256, values, 0)
    lax.fori_loop(0, x_s.shape[0] // 256, keys, 0)


def attend(q_ref, kt_s, v_s, acc_in, acc_out):
    lane_q = lax.broadcasted_iota(jnp.int32, (ROWS, 128), 1) < HEAD
    lane_v = lax.broadcasted_iota(jnp.int32, (kt_s.shape[1], 128), 1) < HEAD
    one = jnp.ones((), BF16)
    zero = jnp.zeros((), BF16)

    def pair(p, carry):
        f = pl.multiple_of(p * 128, 128)
        qp = q_ref[:, pl.ds(f, 128)]
        vp = v_s[:, pl.ds(f, 128)]
        for odd in range(2):
            keep = lane_q if odd == 0 else jnp.logical_not(lane_q)
            keepv = lane_v if odd == 0 else jnp.logical_not(lane_v)
            s = dot(jnp.where(keep, qp, zero), kt_s[pl.ds(f, 128), :])
            total = dot(jnp.exp2(s).astype(BF16), jnp.where(keepv, vp, one))
            if acc_in is not None:
                total = total + acc_in[2 * p + odd]
            acc_out[2 * p + odd] = total
        return carry

    lax.fori_loop(0, PAIRS, pair, 0, unroll=4)


def first_kernel(
    time_ref, ramp_ref, base_ref, l0, l1, l2, l3, p0, p1, p2, p3, gain_ref, shift_ref, w_hbm,
    qgain_ref, kgain_ref, acc_ref, q_ref, first_s, diff_s, x_s, kt_s, v_s, w_ref, sem,
):
    fetch = pltpu.make_async_copy(w_hbm, w_ref, sem)
    fetch.start()
    blend_tables(time_ref, (p0, p1, p2, p3), base_ref, first_s, diff_s)
    for j, lat in enumerate((l0, l1, l2, l3)):
        norm_chunk(j, lat, ramp_ref, 2 * j, first_s, diff_s, gain_ref, shift_ref, x_s)
    fetch.wait()

    def queries(i, carry):
        f = pl.multiple_of(i * 256, 256)
        qt = dot_tt(w_ref[:, pl.ds(f, 256)], x_s[:ROWS, :])
        q_ref[:, pl.ds(f, 256)] = head_norm_t(qt, qgain_ref[...]).T.astype(BF16)
        return carry

    lax.fori_loop(0, D // 256, queries, 0)
    keys_values(x_s, w_ref, kgain_ref, kt_s, v_s)
    attend(q_ref, kt_s, v_s, None, acc_ref)


def second_kernel(
    time_ref, ramp_ref, base_ref, own, l0, l1, l2, l3, p0, p1, p2, p3, gain_ref, shift_ref, w_hbm,
    kgain_ref, wo_ref, q_ref, acc_ref, out_ref, first_s, diff_s, x_s, kt_s, v_s, w_ref, sem, acc_s,
):
    fetch = pltpu.make_async_copy(w_hbm, w_ref, sem)
    fetch.start()
    blend_tables(time_ref, (p0, p1, p2, p3), base_ref, first_s, diff_s)
    for j, lat in enumerate((l0, l1, l2, l3)):
        norm_chunk(j, lat, ramp_ref, 8 + 2 * j, first_s, diff_s, gain_ref, shift_ref, x_s)
    fetch.wait()
    keys_values(x_s, w_ref, kgain_ref, kt_s, v_s)
    attend(q_ref, kt_s, v_s, acc_ref, acc_s)

    lane = lax.broadcasted_iota(jnp.int32, (ROWS, 128), 1) < HEAD
    for p in range(PAIRS):
        even = acc_s[2 * p]
        odd = acc_s[2 * p + 1]
        num = jnp.where(lane, even, odd)
        den = pltpu.roll(jnp.where(lane, odd, even), HEAD, 1)
        x_s[:ROWS, p * 128 : (p + 1) * 128] = (num / den).astype(BF16)

    def block(i, carry):
        f = pl.multiple_of(i * 256, 256)
        o = dot(x_s[:ROWS, :], wo_ref[:, pl.ds(f, 256)])
        for k in range(2):
            r = slice(k * TOKF, (k + 1) * TOKF)
            resid = own[r, pl.ds(f, 256)].astype(F32) + (
                first_s[:, pl.ds(f, 256)] + ramp_ref[16 + k] * diff_s[:, pl.ds(f, 256)]
            )
            out_ref[r, pl.ds(f, 256)] = (resid + o[r]).astype(BF16)
        return carry

    lax.fori_loop(0, D // 256, block, 0)


def mask_kernel(pick_ref, mine, other, *out_refs):
    for t in range(X):
        for k in range(2):
            pick = pick_ref[2 * t + k]

            @pl.when(pick < 0)
            def _():
                out_refs[t][k] = jnp.zeros_like(out_refs[t][k])

            for c, held in enumerate((mine, other)):

                @pl.when(jnp.logical_and(pick >= ZL * c, pick < ZL * (c + 1)))
                def _():
                    out_refs[t][k] = held[pick - ZL * c]


VMEM = pl.BlockSpec(memory_space=pltpu.VMEM)
SMEM = pl.BlockSpec(memory_space=pltpu.SMEM)
HBM = pl.BlockSpec(memory_space=pltpu.HBM)


def scratch():
    return [
        pltpu.VMEM((TOKF, D), F32),
        pltpu.VMEM((TOKF, D), F32),
        pltpu.VMEM((Y * ROWS, D), BF16),
        pltpu.VMEM((D, Y * ROWS), BF16),
        pltpu.VMEM((Y * ROWS, D), BF16),
        pltpu.VMEM((D, 3 * D), BF16),
        pltpu.SemaphoreType.DMA,
    ]


def tables():
    ramps, bases = [], []
    for seq in range(ZH * Y):
        zh, y = divmod(seq, Y)
        near = [2 * (zh * Y + (y - j) % Y) + k for j in range(Y) for k in range(2)]
        far = [2 * ((1 - zh) * Y + (y - j) % Y) + k for j in range(Y) for k in range(2)]
        own = [2 * seq, 2 * seq + 1]
        ramps.append([frame / (FRAMES - 1) for frame in near + far + own])
        base = [(z * Y + (y - j) % Y) * PIECE for j in range(Y) for z in (zh, 1 - zh)]
        bases.append(base + [y])
    return np.array(ramps, np.float32), np.array(bases, np.int32)


def body(
    latents, keyframes, key_index, timesteps, mod_weight, norm_gain, qkv_weight, query_gain,
    key_gain, out_weight,
):
    zl, x, core = lax.axis_index("zl"), lax.axis_index("x"), lax.axis_index("core")
    seq = lax.axis_index("zh") * Y + lax.axis_index("y")

    own = latents.reshape(ROWS, D)
    mine = keyframes[0]
    pair = key_index

    planes = jnp.stack([mine, send(mine, zh=1)])
    near_1 = send(own, y=1)
    near_3 = send(own, y=3)
    by_zl = jnp.stack([planes] + [send(planes, zl=k) for k in (1, 2, 3)])
    pairs = [key_index] + [send(after(key_index, planes), x=k) for k in (1, 2, 3)]
    near_2 = send(after(own, near_1), y=2)
    near = [own, near_1, near_2, near_3]
    cross = send(after(own, by_zl), zh=1)

    wanted = jnp.concatenate(pairs).reshape(-1)
    entry = ((core + wanted) % CORE) * ZL + (zl - wanted // (X * CORE)) % ZL
    picks = jnp.where(wanted // CORE % X == x, entry, -1)
    picks = after(picks, (near_1, near_3))
    masked = pl.pallas_call(
        mask_kernel,
        out_shape=(jax.ShapeDtypeStruct((2, ZH, PIECE, D), BF16),) * X,
        in_specs=[SMEM] + [VMEM] * 2,
        out_specs=(VMEM,) * X,
        name="mask",
    )(picks, by_zl, send(by_zl, core=1))
    found = [send(masked[t], x=X - t) for t in (1, 2, 3)]
    both = after(masked[0], near_2) + found[0] + found[1] + found[2]
    pieces = [both] + [send(both, y=k) for k in (1, 2, 3)]
    late = after(cross, pieces[1])
    far = [cross] + [send(late, y=k) for k in (1, 2, 3)]

    halfway = TEMB // 2
    freqs = jnp.exp(-math.log(10000.0) * jnp.arange(halfway, dtype=F32) / halfway)
    angles = timesteps[1].astype(F32) * freqs
    embed = jnp.concatenate([jnp.sin(angles), jnp.cos(angles)]).astype(BF16)
    modulation = jnp.dot(embed[None, :], mod_weight, preferred_element_type=F32)
    gain = norm_gain[None, :] * (1.0 + modulation[:, :D])
    shift = modulation[:, D:]

    qgain = (query_gain * QSCALE)[:, None]
    kgain = key_gain[:, None]
    ramp_table, base_table = tables()
    ramps = lax.dynamic_index_in_dim(jnp.asarray(ramp_table), seq, 0, keepdims=False)
    base = lax.dynamic_index_in_dim(jnp.asarray(base_table), seq, 0, keepdims=False)

    flops = 2 * 1024 * 1024 * 2048 + 4 * 16 * 256 * 1024 * 128
    params = pltpu.CompilerParams(vmem_limit_bytes=32 * 1024 * 1024)
    acc, q = pl.pallas_call(
        first_kernel,
        out_shape=(
            jax.ShapeDtypeStruct((HEADS, ROWS, 128), F32),
            jax.ShapeDtypeStruct((ROWS, D), BF16),
        ),
        in_specs=[SMEM] * 3 + [VMEM] * 10 + [HBM] + [VMEM] * 2,
        out_specs=(VMEM, VMEM),
        scratch_shapes=scratch(),
        compiler_params=params,
        cost_estimate=pl.CostEstimate(flops=flops, bytes_accessed=12 << 20, transcendentals=4 << 20),
        name="near_keys",
    )(timesteps, ramps, base, *near, *pieces, gain, shift, qkv_weight, qgain, kgain)
    out = pl.pallas_call(
        second_kernel,
        out_shape=jax.ShapeDtypeStruct((ROWS, D), BF16),
        in_specs=[SMEM] * 3 + [VMEM] * 11 + [HBM] + [VMEM] * 4,
        out_specs=VMEM,
        scratch_shapes=scratch() + [pltpu.VMEM((HEADS, ROWS, 128), F32)],
        compiler_params=params,
        cost_estimate=pl.CostEstimate(flops=flops, bytes_accessed=12 << 20, transcendentals=4 << 20),
        name="far_keys",
    )(timesteps, ramps, base, own, *far, *pieces, gain, shift, qkv_weight, kgain, out_weight, q, acc)
    return out.reshape(latents.shape)


def solution(mesh):
    split = Mesh(mesh.devices.reshape(ZL, X, CORE, ZH, Y), AXES)
    leaf, seq = ("zl", "x", "core"), ("zh", "y")
    in_specs = (P(leaf, seq, None, None), P(leaf, seq, None), P(leaf, None)) + (P(),) * 7
    out_specs = P(leaf, seq, None, None)
    return jax.shard_map(body, mesh=split, in_specs=in_specs, out_specs=out_specs, check_vma=False)
```

```python
import math

import jax
import jax.numpy as jnp
from jax import lax
from jax.experimental import pallas as pl
from jax.experimental.pallas import tpu as pltpu
from jax.sharding import Mesh
from jax.sharding import PartitionSpec as P

HEADS = 16
HEAD = 64
TEMB = 256
TSTEPS = 1000
D = 1024
FRAMES = 16
TOKF = 128
AXES = ("zl", "x", "core", "zh", "y")
ZL, X, CORE, ZH, Y = 4, 4, 2, 2, 4
ROWS = 256
PIECE = 16
PAIRS = HEADS // 2
F32 = jnp.float32
BF16 = jnp.bfloat16
QSCALE = HEAD ** (-0.5) * math.log2(math.e)


def moves(zl=0, x=0, core=0, zh=0, y=0):
    pairs = []
    for i in range(ZL * X * CORE * ZH * Y):
        rest, iy = divmod(i, Y)
        rest, izh = divmod(rest, ZH)
        rest, ic = divmod(rest, CORE)
        izl, ix = divmod(rest, X)
        izl, ix, ic = (izl + zl) % ZL, (ix + x) % X, (ic + core) % CORE
        izh, iy = (izh + zh) % ZH, (iy + y) % Y
        pairs.append((i, (((izl * X + ix) * CORE + ic) * ZH + izh) * Y + iy))
    return pairs


def send(value, **step):
    return lax.ppermute(value, AXES, moves(**step))


def after(value, earlier):
    return lax.optimization_barrier((value, earlier))[0]


def dot(a, b):
    return jnp.dot(a, b, preferred_element_type=F32)


def dot_tt(a, b):
    return lax.dot_general(a, b, (((0,), (1,)), ((), ())), preferred_element_type=F32)


def blend_tables(time_ref, pieces, first_s, diff_s):
    zh, y = lax.axis_index("zh"), lax.axis_index("y")
    kw = 1.0 - time_ref[0].astype(F32) * (1.0 / (2.0 * TSTEPS))
    for i, piece in enumerate(pieces):
        for z in range(ZH):
            slot = ((zh + z) % ZH) * Y + (y + Y - i) % Y
            base = pl.multiple_of(slot * PIECE, PIECE)
            first = piece[0, z].astype(F32) * kw
            last = piece[1, z].astype(F32) * kw
            first_s[pl.ds(base, PIECE), :] = first
            diff_s[pl.ds(base, PIECE), :] = last - first


def ramp_of(z, back, which):
    zh, y = lax.axis_index("zh"), lax.axis_index("y")
    frame = 2 * (((zh + z) % ZH) * Y + (y + Y - back) % Y) + which
    return frame.astype(F32) * (1.0 / (FRAMES - 1))


def norm_rows(j, i, step, source, lat_s, x_s, first_s, diff_s, gain_ref, shift_ref):
    rows = pl.ds(pl.multiple_of(j * ROWS + i * step, step), step)
    tok = pl.ds(pl.multiple_of(lax.rem(i, TOKF // step) * step, step), step)
    ramp = ramp_of(*source, i // (TOKF // step))
    resid = lat_s[rows, :].astype(F32) + (first_s[tok, :] + ramp * diff_s[tok, :])
    mean = jnp.mean(resid, axis=-1, keepdims=True)
    cent = resid - mean
    var = jnp.mean(cent * cent, axis=-1, keepdims=True)
    normed = cent * lax.rsqrt(var + 1e-06) * gain_ref[...] + shift_ref[...]
    x_s[rows, :] = normed.astype(BF16)


def norm_chunk(j, source, *refs):
    step = 32

    def rows(i, carry):
        norm_rows(j, i, step, source, *refs)
        return carry

    lax.fori_loop(0, ROWS // step, rows, 0, unroll=4)


def head_norm_t(block, gain):
    heads = block.reshape(block.shape[0] // HEAD, HEAD, block.shape[1])
    mean = jnp.mean(heads * heads, axis=1, keepdims=True)
    return (heads * lax.rsqrt(mean + 1e-06) * gain[None]).reshape(block.shape)


def keys_values(x_s, w_ref, kgain_ref, kt_s, v_s):
    rows = x_s.shape[0]
    wide = 512 if rows % 512 == 0 else 256

    def values(i, carry):
        f = pl.multiple_of(i * 512, 512)
        v_s[:, pl.ds(f, 512)] = dot(x_s[...], w_ref[:, pl.ds(2 * D + f, 512)]).astype(BF16)
        return carry

    def keys(i, carry):
        t = pl.multiple_of(i * wide, wide)
        kt = dot_tt(w_ref[:, D : 2 * D], x_s[pl.ds(t, wide), :])
        kt_s[:, pl.ds(t, wide)] = head_norm_t(kt, kgain_ref[...]).astype(BF16)
        return carry

    lax.fori_loop(0, rows // wide, keys, 0)
    lax.fori_loop(0, D // 512, values, 0)


def attend(q_s, kt_s, v_s, use):
    lane = lax.broadcasted_iota(jnp.int32, (ROWS, 128), 1) < HEAD
    lane_v = lax.broadcasted_iota(jnp.int32, (kt_s.shape[1], 128), 1) < HEAD
    one = jnp.ones((), BF16)
    zero = jnp.zeros((), BF16)

    def pair(p, carry):
        f = pl.multiple_of(p * 128, 128)
        qp = q_s[:, pl.ds(f, 128)]
        vp = v_s[:, pl.ds(f, 128)]
        kt = kt_s[pl.ds(f, 128), :]
        even = dot(
            jnp.exp2(dot(jnp.where(lane, qp, zero), kt)).astype(BF16), jnp.where(lane_v, vp, one)
        )
        odd = dot(
            jnp.exp2(dot(jnp.where(lane, zero, qp), kt)).astype(BF16), jnp.where(lane_v, one, vp)
        )
        use(p, even, odd)
        return carry

    lax.fori_loop(0, PAIRS, pair, 0, unroll=4)


def prepare(time_ref, lats, sources, pieces, gain_ref, shift_ref, rest, scr):
    piece_s, lat_s, first_s, diff_s, x_s, sems = scr
    targets = [piece_s.at[i] for i in range(len(pieces))]
    targets += [lat_s.at[pl.ds(j * ROWS, ROWS)] for j in range(len(lats))]
    copies = [
        pltpu.make_async_copy(source, target, sems.at[i])
        for i, (source, target) in enumerate(zip(pieces + lats, targets))
    ]
    for copy in copies + rest:
        copy.start()
    for copy in copies[: len(pieces)]:
        copy.wait()
    blend_tables(time_ref, targets[: len(pieces)], first_s, diff_s)
    for j in range(len(lats)):
        copies[len(pieces) + j].wait()
        norm_chunk(j, sources[j], lat_s, x_s, first_s, diff_s, gain_ref, shift_ref)


def prelude_kernel(embed_ref, mod_ref, norm_ref, qgain_ref, kgain_ref, w_ref, wo_ref, *out_refs):
    gain, shift, qgain, kgain = out_refs
    embed = jnp.broadcast_to(embed_ref[...], (16, TEMB))
    modulation = dot(embed, mod_ref[...])
    gain[...] = norm_ref[...] * (1.0 + modulation[:1, :D])
    shift[...] = modulation[:1, D:]
    qgain[...] = jnp.broadcast_to(qgain_ref[...] * QSCALE, (8, HEAD)).T[:, :1]
    kgain[...] = jnp.broadcast_to(kgain_ref[...], (8, HEAD)).T[:, :1]


def near_kernel(
    time_ref, l0, l1, l2, l3, l4, p0, p1, p2, p3, gain_ref, shift_ref, w_ref, qgain_ref, kgain_ref,
    acc_ref, q_ref, piece_s, lat_s, first_s, diff_s, x_s, sems, kt_s, v_s,
):
    prepare(
        time_ref, (l0, l1, l2, l3, l4), ((0, 0), (0, 1), (0, 2), (0, 3), (1, 0)), (p0, p1, p2, p3),
        gain_ref, shift_ref, [], (piece_s, lat_s, first_s, diff_s, x_s, sems),
    )
    qt = head_norm_t(dot_tt(w_ref[:, :D], x_s[:ROWS, :]), qgain_ref[...])
    q_ref[...] = qt.astype(BF16).T
    keys_values(x_s, w_ref, kgain_ref, kt_s, v_s)

    def use(p, even, odd):
        acc_ref[2 * p] = even
        acc_ref[2 * p + 1] = odd

    attend(q_ref, kt_s, v_s, use)


def far_kernel(
    time_ref, own, l0, l1, l2, p0, p1, p2, p3, gain_ref, shift_ref, w_ref, kgain_ref, wo_ref, q_ref,
    acc_ref, out_ref, piece_s, lat_s, first_s, diff_s, x_s, sems, kt_s, v_s, own_s, att_s, own_sem,
):
    rest = [pltpu.make_async_copy(own, own_s, own_sem)]
    prepare(
        time_ref, (l0, l1, l2), ((1, 1), (1, 2), (1, 3)), (p0, p1, p2, p3), gain_ref, shift_ref,
        rest, (piece_s, lat_s, first_s, diff_s, x_s, sems),
    )
    keys_values(x_s, w_ref, kgain_ref, kt_s, v_s)
    for copy in rest:
        copy.wait()
    lane = lax.broadcasted_iota(jnp.int32, (ROWS, 128), 1) < HEAD

    def use(p, even, odd):
        even = even + acc_ref[2 * p]
        odd = odd + acc_ref[2 * p + 1]
        total = pltpu.roll(jnp.where(lane, odd, even), HEAD, 1)
        f = pl.multiple_of(p * 128, 128)
        att_s[:, pl.ds(f, 128)] = (jnp.where(lane, even, odd) / total).astype(BF16)

    attend(q_ref, kt_s, v_s, use)

    def block(i, carry):
        f = pl.multiple_of(i * 256, 256)
        o = dot(att_s[...], wo_ref[:, pl.ds(f, 256)])
        for k in range(2):
            r = slice(k * TOKF, (k + 1) * TOKF)
            resid = own_s[r, pl.ds(f, 256)].astype(F32) + (
                first_s[:, pl.ds(f, 256)] + ramp_of(0, 0, k) * diff_s[:, pl.ds(f, 256)]
            )
            out_ref[r, pl.ds(f, 256)] = (resid + o[r]).astype(BF16)
        return carry

    lax.fori_loop(0, D // 256, block, 0)


def pick_kernel(pair_ref, other_ref, x0, x1, x2, x3, *out_refs):
    zl, x, core = lax.axis_index("zl"), lax.axis_index("x"), lax.axis_index("core")
    for wants, out_ref in zip((pair_ref, other_ref), out_refs):
        for k in range(2):
            wanted = wants[0, k]
            back = (x + X - wanted // CORE % X) % X
            entry = (zl + ZL - wanted // (X * CORE)) % ZL
            back = jnp.where(wanted % CORE == core, back, -1)

            @pl.when(back < 0)
            def _():
                out_ref[k] = jnp.zeros_like(out_ref[k])

            for t, held in enumerate((x0, x1, x2, x3)):

                @pl.when(back == t)
                def _():
                    out_ref[k] = held[entry]


VMEM = pl.BlockSpec(memory_space=pltpu.VMEM)
LIMIT = 32 * 1024 * 1024
SMEM = pl.BlockSpec(memory_space=pltpu.SMEM)
HBM = pl.BlockSpec(memory_space=pltpu.HBM)


def scratch(chunks):
    rows = chunks * ROWS
    return [
        pltpu.VMEM((Y, 2, ZH, PIECE, D), BF16),
        pltpu.VMEM((rows, D), BF16),
        pltpu.VMEM((TOKF, D), F32),
        pltpu.VMEM((TOKF, D), F32),
        pltpu.VMEM((rows, D), BF16),
        pltpu.SemaphoreType.DMA((Y + chunks,)),
        pltpu.VMEM((D, rows), BF16),
        pltpu.VMEM((rows, D), BF16),
    ]


def body(
    latents, keyframes, key_index, timesteps, mod_weight, norm_gain, qkv_weight, query_gain,
    key_gain, out_weight,
):
    own = latents.reshape(ROWS, D)
    mine = keyframes[0]
    pair = key_index

    near_1, near_3 = send(own, y=1), send(own, y=3)
    pair_other = send(key_index, core=1)
    planes = jnp.stack([after(mine, pair_other), send(mine, zh=1)])
    from_zl = [send(planes, zl=k) for k in (1, 2, 3)]
    by_zl = jnp.stack([planes] + from_zl)
    by_x = [by_zl] + [send(by_zl, x=k) for k in (1, 2, 3)]
    cross = send(after(own, from_zl), zh=1)
    near_2 = send(after(own, near_3), y=2)
    picked = jax.ShapeDtypeStruct((2, ZH, PIECE, D), BF16)
    held, asked = pl.pallas_call(
        pick_kernel,
        out_shape=(picked, picked),
        in_specs=[SMEM] * 2 + [VMEM] * 4,
        out_specs=(VMEM, VMEM),
        name="pick",
    )(key_index, after(pair_other, (near_1, near_3)), *by_x)
    both = after(held, near_2) + send(asked, core=1)
    pieces = [both] + [send(both, y=k) for k in (1, 2, 3)]
    late = after(cross, both)
    far_1, far_2, far_3 = [send(late, y=k) for k in (1, 2, 3)]

    halfway = TEMB // 2
    freqs = jnp.exp(-math.log(10000.0) * jnp.arange(halfway, dtype=F32) / halfway)
    angles = timesteps[1].astype(F32) * freqs
    embed = jnp.concatenate([jnp.sin(angles), jnp.cos(angles)]).astype(BF16)[None, :]
    gain, shift, qgain, kgain = pl.pallas_call(
        prelude_kernel,
        out_shape=(jax.ShapeDtypeStruct((1, D), F32),) * 2 + (jax.ShapeDtypeStruct((HEAD, 1), F32),) * 2,
        in_specs=[VMEM] * 7,
        out_specs=(VMEM,) * 4,
        compiler_params=pltpu.CompilerParams(vmem_limit_bytes=LIMIT),
        name="prelude",
    )(
        embed, mod_weight, norm_gain[None, :], query_gain[None, :], key_gain[None, :], qkv_weight,
        out_weight,
    )

    params = pltpu.CompilerParams(vmem_limit_bytes=LIMIT)
    cost = pl.CostEstimate(flops=6 << 30, bytes_accessed=12 << 20, transcendentals=4 << 20)
    acc, q = pl.pallas_call(
        near_kernel,
        out_shape=(
            jax.ShapeDtypeStruct((HEADS, ROWS, 128), F32),
            jax.ShapeDtypeStruct((ROWS, D), BF16),
        ),
        in_specs=[SMEM] + [HBM] * 9 + [VMEM] * 5,
        out_specs=(VMEM, VMEM),
        scratch_shapes=scratch(5),
        compiler_params=params,
        cost_estimate=cost,
        name="near_keys",
    )(
        timesteps, own, near_1, near_2, near_3, cross, *pieces, gain, shift,
        qkv_weight, qgain, kgain,
    )
    out = pl.pallas_call(
        far_kernel,
        out_shape=jax.ShapeDtypeStruct((ROWS, D), BF16),
        in_specs=[SMEM] + [HBM] * 8 + [VMEM] * 7,
        out_specs=VMEM,
        scratch_shapes=scratch(3) + [
            pltpu.VMEM((ROWS, D), BF16),
            pltpu.VMEM((ROWS, D), BF16),
            pltpu.SemaphoreType.DMA,
        ],
        compiler_params=params,
        cost_estimate=cost,
        name="far_keys",
    )(
        timesteps, own, far_1, far_2, far_3, *pieces, gain, shift, qkv_weight, kgain,
        out_weight, q, acc,
    )
    return out.reshape(latents.shape)


def solution(mesh):
    split = Mesh(mesh.devices.reshape(ZL, X, CORE, ZH, Y), AXES)
    leaf, seq = ("zl", "x", "core"), ("zh", "y")
    in_specs = (P(leaf, seq, None, None), P(leaf, seq, None), P(leaf, None)) + (P(),) * 7
    out_specs = P(leaf, seq, None, None)
    return jax.shard_map(body, mesh=split, in_specs=in_specs, out_specs=out_specs, check_vma=False)
```

```python
import math

import jax
import jax.numpy as jnp
from jax import lax
from jax.experimental import pallas as pl
from jax.experimental.pallas import tpu as pltpu
from jax.sharding import Mesh
from jax.sharding import PartitionSpec as P

HEADS = 16
HEAD = 64
TEMB = 256
TSTEPS = 1000
D = 1024
FRAMES = 16
TOKF = 128
AXES = ("zl", "x", "core", "zh", "y")
ZL, X, CORE, ZH, Y = 4, 4, 2, 2, 4
ROWS = 256
PIECE = 16
PAIRS = HEADS // 2
F32 = jnp.float32
BF16 = jnp.bfloat16
QSCALE = HEAD ** (-0.5) * math.log2(math.e)


def moves(zl=0, x=0, core=0, zh=0, y=0):
    pairs = []
    for i in range(ZL * X * CORE * ZH * Y):
        rest, iy = divmod(i, Y)
        rest, izh = divmod(rest, ZH)
        rest, ic = divmod(rest, CORE)
        izl, ix = divmod(rest, X)
        izl, ix, ic = (izl + zl) % ZL, (ix + x) % X, (ic + core) % CORE
        izh, iy = (izh + zh) % ZH, (iy + y) % Y
        pairs.append((i, (((izl * X + ix) * CORE + ic) * ZH + izh) * Y + iy))
    return pairs


def send(value, **step):
    return lax.ppermute(value, AXES, moves(**step))


def after(value, earlier):
    return lax.optimization_barrier((value, earlier))[0]


def dot(a, b):
    return jnp.dot(a, b, preferred_element_type=F32)


def dot_tt(a, b):
    return lax.dot_general(a, b, (((0,), (1,)), ((), ())), preferred_element_type=F32)


def blend_tables(time_ref, pieces, first_s, diff_s):
    zh, y = lax.axis_index("zh"), lax.axis_index("y")
    kw = 1.0 - time_ref[0].astype(F32) * (1.0 / (2.0 * TSTEPS))
    for i, piece in enumerate(pieces):
        for z in range(ZH):
            slot = ((zh + z) % ZH) * Y + (y + Y - i) % Y
            base = pl.multiple_of(slot * PIECE, PIECE)
            first = piece[0, z].astype(F32) * kw
            last = piece[1, z].astype(F32) * kw
            first_s[pl.ds(base, PIECE), :] = first
            diff_s[pl.ds(base, PIECE), :] = last - first


def ramp_of(z, back, which):
    zh, y = lax.axis_index("zh"), lax.axis_index("y")
    frame = 2 * (((zh + z) % ZH) * Y + (y + Y - back) % Y) + which
    return frame.astype(F32) * (1.0 / (FRAMES - 1))


def norm_rows(j, i, step, source, lat_s, x_s, first_s, diff_s, gain_ref, shift_ref):
    rows = pl.ds(pl.multiple_of(j * ROWS + i * step, step), step)
    tok = pl.ds(pl.multiple_of(lax.rem(i, TOKF // step) * step, step), step)
    ramp = ramp_of(*source, i // (TOKF // step))
    resid = lat_s[rows, :].astype(F32) + (first_s[tok, :] + ramp * diff_s[tok, :])
    mean = jnp.mean(resid, axis=-1, keepdims=True)
    cent = resid - mean
    var = jnp.mean(cent * cent, axis=-1, keepdims=True)
    normed = cent * lax.rsqrt(var + 1e-06) * gain_ref[...] + shift_ref[...]
    x_s[rows, :] = normed.astype(BF16)


def norm_chunk(j, source, *refs):
    step = 32

    def rows(i, carry):
        norm_rows(j, i, step, source, *refs)
        return carry

    lax.fori_loop(0, ROWS // step, rows, 0, unroll=8)


def head_norm_t(block, gain):
    heads = block.reshape(block.shape[0] // HEAD, HEAD, block.shape[1])
    mean = jnp.mean(heads * heads, axis=1, keepdims=True)
    return (heads * lax.rsqrt(mean + 1e-06) * gain[None]).reshape(block.shape)


def keys_values(x_s, w_ref, kgain_ref, kt_s, v_s):
    kt = dot_tt(w_ref[:, D : 2 * D], x_s[...])
    kt_s[...] = head_norm_t(kt, kgain_ref[...]).astype(BF16)
    v_s[...] = dot(x_s[...], w_ref[:, 2 * D :]).astype(BF16)


def attend(q_s, kt_s, v_s, use, unroll):
    lane = lax.broadcasted_iota(jnp.int32, (ROWS, 128), 1) < HEAD
    lane_v = lax.broadcasted_iota(jnp.int32, (kt_s.shape[1], 128), 1) < HEAD
    one = jnp.ones((), BF16)
    zero = jnp.zeros((), BF16)

    def pair(p, carry):
        f = pl.multiple_of(p * 128, 128)
        qp = q_s[:, pl.ds(f, 128)]
        vp = v_s[:, pl.ds(f, 128)]
        kt = kt_s[pl.ds(f, 128), :]
        even = dot(
            jnp.exp2(dot(jnp.where(lane, qp, zero), kt)).astype(BF16), jnp.where(lane_v, vp, one)
        )
        odd = dot(
            jnp.exp2(dot(jnp.where(lane, zero, qp), kt)).astype(BF16), jnp.where(lane_v, one, vp)
        )
        use(p, even, odd)
        return carry

    lax.fori_loop(0, PAIRS, pair, 0, unroll=unroll)


def prepare(time_ref, lats, sources, pieces, gain_ref, shift_ref, rest, scr):
    piece_s, lat_s, first_s, diff_s, x_s, sems = scr
    targets = [piece_s.at[i] for i in range(len(pieces))]
    targets += [lat_s.at[pl.ds(j * ROWS, ROWS)] for j in range(len(lats))]
    copies = [
        pltpu.make_async_copy(source, target, sems.at[i])
        for i, (source, target) in enumerate(zip(pieces + lats, targets))
    ]
    for copy in copies + rest:
        copy.start()
    for copy in copies[: len(pieces)]:
        copy.wait()
    blend_tables(time_ref, targets[: len(pieces)], first_s, diff_s)
    for j in range(len(lats)):
        copies[len(pieces) + j].wait()
        norm_chunk(j, sources[j], lat_s, x_s, first_s, diff_s, gain_ref, shift_ref)


def prelude_kernel(embed_ref, mod_ref, norm_ref, qgain_ref, kgain_ref, w_ref, wo_ref, *out_refs):
    gain, shift, qgain, kgain = out_refs
    embed = jnp.broadcast_to(embed_ref[...], (16, TEMB))
    modulation = dot(embed, mod_ref[...])
    gain[...] = norm_ref[...] * (1.0 + modulation[:1, :D])
    shift[...] = modulation[:1, D:]
    qgain[...] = jnp.broadcast_to(qgain_ref[...] * QSCALE, (8, HEAD)).T[:, :1]
    kgain[...] = jnp.broadcast_to(kgain_ref[...], (8, HEAD)).T[:, :1]


def first_kernel(
    time_ref, l0, l1, l2, p0, p1, p2, p3, gain_ref, shift_ref, w_ref, qgain_ref, kgain_ref,
    acc_ref, q_ref, piece_s, lat_s, first_s, diff_s, x_s, sems, kt_s, v_s,
):
    prepare(
        time_ref, (l0, l1, l2), ((0, 0), (0, 1), (0, 3)), (p0, p1, p2, p3),
        gain_ref, shift_ref, [], (piece_s, lat_s, first_s, diff_s, x_s, sems),
    )
    qt = head_norm_t(dot_tt(w_ref[:, :D], x_s[:ROWS, :]), qgain_ref[...])
    q_ref[...] = qt.astype(BF16).T
    keys_values(x_s, w_ref, kgain_ref, kt_s, v_s)

    def use(p, even, odd):
        acc_ref[2 * p] = even
        acc_ref[2 * p + 1] = odd

    attend(q_ref, kt_s, v_s, use, 8)


def middle_kernel(
    time_ref, l0, l1, l2, l3, p0, p1, p2, p3, gain_ref, shift_ref, w_ref, kgain_ref, q_ref, acc_ref,
    sum_ref, piece_s, lat_s, first_s, diff_s, x_s, sems, kt_s, v_s,
):
    prepare(
        time_ref, (l0, l1, l2, l3), ((0, 2), (1, 0), (1, 1), (1, 3)), (p0, p1, p2, p3),
        gain_ref, shift_ref, [], (piece_s, lat_s, first_s, diff_s, x_s, sems),
    )
    keys_values(x_s, w_ref, kgain_ref, kt_s, v_s)

    def use(p, even, odd):
        sum_ref[2 * p] = even + acc_ref[2 * p]
        sum_ref[2 * p + 1] = odd + acc_ref[2 * p + 1]

    attend(q_ref, kt_s, v_s, use, 8)


def last_kernel(
    time_ref, own, l0, p0, p1, p2, p3, gain_ref, shift_ref, w_ref, kgain_ref, wo_ref, q_ref,
    acc_ref, out_ref, piece_s, lat_s, first_s, diff_s, x_s, sems, kt_s, v_s, own_s, att_s, own_sem,
):
    rest = [pltpu.make_async_copy(own, own_s, own_sem)]
    prepare(
        time_ref, (l0,), ((1, 2),), (p0, p1, p2, p3), gain_ref, shift_ref,
        rest, (piece_s, lat_s, first_s, diff_s, x_s, sems),
    )
    keys_values(x_s, w_ref, kgain_ref, kt_s, v_s)
    for copy in rest:
        copy.wait()
    lane = lax.broadcasted_iota(jnp.int32, (ROWS, 128), 1) < HEAD

    def use(p, even, odd):
        even = even + acc_ref[2 * p]
        odd = odd + acc_ref[2 * p + 1]
        total = pltpu.roll(jnp.where(lane, odd, even), HEAD, 1)
        f = pl.multiple_of(p * 128, 128)
        att_s[:, pl.ds(f, 128)] = (jnp.where(lane, even, odd) / total).astype(BF16)

    attend(q_ref, kt_s, v_s, use, 4)

    def block(i, carry):
        f = pl.multiple_of(i * 256, 256)
        o = dot(att_s[...], wo_ref[:, pl.ds(f, 256)])
        for k in range(2):
            r = slice(k * TOKF, (k + 1) * TOKF)
            resid = own_s[r, pl.ds(f, 256)].astype(F32) + (
                first_s[:, pl.ds(f, 256)] + ramp_of(0, 0, k) * diff_s[:, pl.ds(f, 256)]
            )
            out_ref[r, pl.ds(f, 256)] = (resid + o[r]).astype(BF16)
        return carry

    lax.fori_loop(0, D // 256, block, 0)


def pick_kernel(pair_ref, other_ref, x0, x1, x2, x3, *out_refs):
    zl, x, core = lax.axis_index("zl"), lax.axis_index("x"), lax.axis_index("core")
    for wants, out_ref in zip((pair_ref, other_ref), out_refs):
        for k in range(2):
            wanted = wants[0, k]
            back = (x + X - wanted // CORE % X) % X
            entry = (zl + ZL - wanted // (X * CORE)) % ZL
            back = jnp.where(wanted % CORE == core, back, -1)

            @pl.when(back < 0)
            def _():
                out_ref[k] = jnp.zeros_like(out_ref[k])

            for t, held in enumerate((x0, x1, x2, x3)):

                @pl.when(back == t)
                def _():
                    out_ref[k] = held[entry]


VMEM = pl.BlockSpec(memory_space=pltpu.VMEM)
LIMIT = 32 * 1024 * 1024
SMEM = pl.BlockSpec(memory_space=pltpu.SMEM)
HBM = pl.BlockSpec(memory_space=pltpu.HBM)


def scratch(chunks):
    rows = chunks * ROWS
    return [
        pltpu.VMEM((Y, 2, ZH, PIECE, D), BF16),
        pltpu.VMEM((rows, D), BF16),
        pltpu.VMEM((TOKF, D), F32),
        pltpu.VMEM((TOKF, D), F32),
        pltpu.VMEM((rows, D), BF16),
        pltpu.SemaphoreType.DMA((Y + chunks,)),
        pltpu.VMEM((D, rows), BF16),
        pltpu.VMEM((rows, D), BF16),
    ]


def body(
    latents, keyframes, key_index, timesteps, mod_weight, norm_gain, qkv_weight, query_gain,
    key_gain, out_weight,
):
    own = latents.reshape(ROWS, D)
    mine = keyframes[0]
    pair = key_index

    near_1, near_3 = send(own, y=1), send(own, y=3)
    pair_other = send(key_index, core=1)
    planes = jnp.stack([after(mine, pair_other), send(mine, zh=1)])
    from_zl = [send(planes, zl=k) for k in (1, 2, 3)]
    by_zl = jnp.stack([planes] + from_zl)
    by_x = [by_zl] + [send(by_zl, x=k) for k in (1, 2, 3)]
    cross = send(after(own, from_zl), zh=1)
    near_2 = send(after(own, (near_1, near_3)), y=2)
    picked = jax.ShapeDtypeStruct((2, ZH, PIECE, D), BF16)
    held, asked = pl.pallas_call(
        pick_kernel,
        out_shape=(picked, picked),
        in_specs=[SMEM] * 2 + [VMEM] * 4,
        out_specs=(VMEM, VMEM),
        name="pick",
    )(key_index, after(pair_other, (near_1, near_3)), *by_x)
    both = after(held, near_2) + send(asked, core=1)
    pieces = [both] + [send(both, y=k) for k in (1, 2, 3)]
    far_1, far_3 = [send(after(cross, both), y=k) for k in (1, 3)]

    halfway = TEMB // 2
    freqs = jnp.exp(-math.log(10000.0) * jnp.arange(halfway, dtype=F32) / halfway)
    angles = timesteps[1].astype(F32) * freqs
    embed = jnp.concatenate([jnp.sin(angles), jnp.cos(angles)]).astype(BF16)[None, :]
    gain, shift, qgain, kgain = pl.pallas_call(
        prelude_kernel,
        out_shape=(jax.ShapeDtypeStruct((1, D), F32),) * 2 + (jax.ShapeDtypeStruct((HEAD, 1), F32),) * 2,
        in_specs=[VMEM] * 7,
        out_specs=(VMEM,) * 4,
        compiler_params=pltpu.CompilerParams(vmem_limit_bytes=LIMIT),
        name="prelude",
    )(
        embed, mod_weight, norm_gain[None, :], query_gain[None, :], key_gain[None, :], qkv_weight,
        out_weight,
    )

    params = pltpu.CompilerParams(vmem_limit_bytes=LIMIT)
    cost = pl.CostEstimate(flops=4 << 30, bytes_accessed=8 << 20, transcendentals=3 << 20)
    sums = jax.ShapeDtypeStruct((HEADS, ROWS, 128), F32)
    token = jax.ShapeDtypeStruct((ROWS, D), BF16)
    acc, q = pl.pallas_call(
        first_kernel,
        out_shape=(sums, token),
        in_specs=[SMEM] + [HBM] * 7 + [VMEM] * 5,
        out_specs=(VMEM, VMEM),
        scratch_shapes=scratch(3),
        compiler_params=params,
        cost_estimate=cost,
        name="first_keys",
    )(timesteps, own, near_1, near_3, *pieces, gain, shift, qkv_weight, qgain, kgain)
    far_2 = send(after(cross, acc), y=2)
    acc = pl.pallas_call(
        middle_kernel,
        out_shape=sums,
        in_specs=[SMEM] + [HBM] * 8 + [VMEM] * 6,
        out_specs=VMEM,
        scratch_shapes=scratch(4),
        compiler_params=params,
        cost_estimate=cost,
        name="middle_keys",
    )(
        timesteps, near_2, cross, far_1, far_3, *pieces, gain, shift, qkv_weight, kgain, q, acc,
    )
    out = pl.pallas_call(
        last_kernel,
        out_shape=token,
        in_specs=[SMEM] + [HBM] * 6 + [VMEM] * 7,
        out_specs=VMEM,
        scratch_shapes=scratch(1) + [
            pltpu.VMEM((ROWS, D), BF16),
            pltpu.VMEM((ROWS, D), BF16),
            pltpu.SemaphoreType.DMA,
        ],
        compiler_params=params,
        cost_estimate=cost,
        name="last_keys",
    )(
        timesteps, own, far_2, *pieces, gain, shift, qkv_weight, kgain, out_weight, q, acc,
    )
    return out.reshape(latents.shape)


def solution(mesh):
    split = Mesh(mesh.devices.reshape(ZL, X, CORE, ZH, Y), AXES)
    leaf, seq = ("zl", "x", "core"), ("zh", "y")
    in_specs = (P(leaf, seq, None, None), P(leaf, seq, None), P(leaf, None)) + (P(),) * 7
    out_specs = P(leaf, seq, None, None)
    return jax.shard_map(body, mesh=split, in_specs=in_specs, out_specs=out_specs, check_vma=False)
```

```python
import math

import jax
import jax.numpy as jnp
from jax import lax
from jax.experimental import pallas as pl
from jax.experimental.pallas import tpu as pltpu
from jax.sharding import Mesh
from jax.sharding import PartitionSpec as P

HEADS = 16
HEAD = 64
TEMB = 256
TSTEPS = 1000
D = 1024
FRAMES = 16
TOKF = 128
AXES = ("zl", "x", "core", "zh", "y")
ZL, X, CORE, ZH, Y = 4, 4, 2, 2, 4
ROWS = 256
PIECE = 16
PAIRS = HEADS // 2
F32 = jnp.float32
BF16 = jnp.bfloat16
QSCALE = HEAD ** (-0.5) * math.log2(math.e)


def moves(zl=0, x=0, core=0, zh=0, y=0):
    pairs = []
    for i in range(ZL * X * CORE * ZH * Y):
        rest, iy = divmod(i, Y)
        rest, izh = divmod(rest, ZH)
        rest, ic = divmod(rest, CORE)
        izl, ix = divmod(rest, X)
        izl, ix, ic = (izl + zl) % ZL, (ix + x) % X, (ic + core) % CORE
        izh, iy = (izh + zh) % ZH, (iy + y) % Y
        pairs.append((i, (((izl * X + ix) * CORE + ic) * ZH + izh) * Y + iy))
    return pairs


def send(value, **step):
    return lax.ppermute(value, AXES, moves(**step))


def after(value, earlier):
    return lax.optimization_barrier((value, earlier))[0]


def dot(a, b):
    return jnp.dot(a, b, preferred_element_type=F32)


def dot_tt(a, b):
    return lax.dot_general(a, b, (((0,), (1,)), ((), ())), preferred_element_type=F32)


def blend_tables(time_ref, pieces, first_s, diff_s):
    zh, y = lax.axis_index("zh"), lax.axis_index("y")
    kw = 1.0 - time_ref[0].astype(F32) * (1.0 / (2.0 * TSTEPS))
    for i, piece in enumerate(pieces):
        for z in range(ZH):
            slot = ((zh + z) % ZH) * Y + (y + Y - i) % Y
            base = pl.multiple_of(slot * PIECE, PIECE)
            first = piece[0, z].astype(F32) * kw
            last = piece[1, z].astype(F32) * kw
            first_s[pl.ds(base, PIECE), :] = first
            diff_s[pl.ds(base, PIECE), :] = last - first


def ramp_of(z, back, which):
    zh, y = lax.axis_index("zh"), lax.axis_index("y")
    frame = 2 * (((zh + z) % ZH) * Y + (y + Y - back) % Y) + which
    return frame.astype(F32) * (1.0 / (FRAMES - 1))


def norm_rows(j, i, step, source, lat_s, x_s, first_s, diff_s, gain_ref, shift_ref):
    rows = pl.ds(pl.multiple_of(j * ROWS + i * step, step), step)
    tok = pl.ds(pl.multiple_of(lax.rem(i, TOKF // step) * step, step), step)
    ramp = ramp_of(*source, i // (TOKF // step))
    resid = lat_s[rows, :].astype(F32) + (first_s[tok, :] + ramp * diff_s[tok, :])
    mean = jnp.mean(resid, axis=-1, keepdims=True)
    cent = resid - mean
    var = jnp.mean(cent * cent, axis=-1, keepdims=True)
    normed = cent * lax.rsqrt(var + 1e-06) * gain_ref[...] + shift_ref[...]
    x_s[rows, :] = normed.astype(BF16)


def norm_chunk(j, source, *refs):
    step = 32

    def rows(i, carry):
        norm_rows(j, i, step, source, *refs)
        return carry

    lax.fori_loop(0, ROWS // step, rows, 0, unroll=8)


def head_norm_t(block, gain):
    heads = block.reshape(block.shape[0] // HEAD, HEAD, block.shape[1])
    mean = jnp.mean(heads * heads, axis=1, keepdims=True)
    return (heads * lax.rsqrt(mean + 1e-06) * gain[None]).reshape(block.shape)


def keys_values(x_s, w_ref, kgain_ref, kt_s, v_s):
    kt = dot_tt(w_ref[:, D : 2 * D], x_s[...])
    kt_s[...] = head_norm_t(kt, kgain_ref[...]).astype(BF16)
    v_s[...] = dot(x_s[...], w_ref[:, 2 * D :]).astype(BF16)


def attend(q_s, kt_s, v_s, use, unroll):
    lane = lax.broadcasted_iota(jnp.int32, (ROWS, 128), 1) < HEAD
    lane_v = lax.broadcasted_iota(jnp.int32, (kt_s.shape[1], 128), 1) < HEAD
    one = jnp.ones((), BF16)
    zero = jnp.zeros((), BF16)

    def pair(p, carry):
        f = pl.multiple_of(p * 128, 128)
        qp = q_s[:, pl.ds(f, 128)]
        vp = v_s[:, pl.ds(f, 128)]
        kt = kt_s[pl.ds(f, 128), :]
        even = dot(
            jnp.exp2(dot(jnp.where(lane, qp, zero), kt)).astype(BF16), jnp.where(lane_v, vp, one)
        )
        odd = dot(
            jnp.exp2(dot(jnp.where(lane, zero, qp), kt)).astype(BF16), jnp.where(lane_v, one, vp)
        )
        use(p, even, odd)
        return carry

    lax.fori_loop(0, PAIRS, pair, 0, unroll=unroll)


def prepare(lats, sources, first, diff, gain_ref, shift_ref, copies, scr, between):
    lat_s, x_s, sems = scr
    lat_copies = [
        pltpu.make_async_copy(lat, lat_s.at[pl.ds(j * ROWS, ROWS)], sems.at[j])
        for j, lat in enumerate(lats)
    ]
    for copy in copies + lat_copies:
        copy.start()
    between()
    for j, copy in enumerate(lat_copies):
        copy.wait()
        norm_chunk(j, sources[j], lat_s, x_s, first, diff, gain_ref, shift_ref)


def prelude_kernel(embed_ref, mod_ref, norm_ref, qgain_ref, kgain_ref, w_ref, wo_ref, *out_refs):
    gain, shift, qgain, kgain = out_refs
    embed = jnp.broadcast_to(embed_ref[...], (16, TEMB))
    modulation = dot(embed, mod_ref[...])
    gain[...] = norm_ref[...] * (1.0 + modulation[:1, :D])
    shift[...] = modulation[:1, D:]
    qgain[...] = jnp.broadcast_to(qgain_ref[...] * QSCALE, (8, HEAD)).T[:, :1]
    kgain[...] = jnp.broadcast_to(kgain_ref[...], (8, HEAD)).T[:, :1]


def first_kernel(
    time_ref, l0, l1, l2, p0, p1, p2, p3, gain_ref, shift_ref, w_ref, qgain_ref, kgain_ref,
    acc_ref, q_ref, first, diff, lat_s, x_s, sems, kt_s, v_s, piece_s, piece_sems,
):
    copies = [
        pltpu.make_async_copy(piece, piece_s.at[i], piece_sems.at[i])
        for i, piece in enumerate((p0, p1, p2, p3))
    ]

    def between():
        for copy in copies:
            copy.wait()
        blend_tables(time_ref, [piece_s.at[i] for i in range(Y)], first, diff)

    prepare(
        (l0, l1, l2), ((0, 0), (0, 1), (0, 3)), first, diff, gain_ref, shift_ref, copies,
        (lat_s, x_s, sems), between,
    )
    qt = head_norm_t(dot_tt(w_ref[:, :D], x_s[:ROWS, :]), qgain_ref[...])
    q_ref[...] = qt.astype(BF16).T
    keys_values(x_s, w_ref, kgain_ref, kt_s, v_s)

    def use(p, even, odd):
        acc_ref[2 * p] = even
        acc_ref[2 * p + 1] = odd

    attend(q_ref, kt_s, v_s, use, 8)


def middle_kernel(
    l0, l1, l2, l3, first, diff, gain_ref, shift_ref, w_ref, kgain_ref, q_ref, acc_ref, sum_ref,
    lat_s, x_s, sems, kt_s, v_s,
):
    prepare(
        (l0, l1, l2, l3), ((0, 2), (1, 0), (1, 1), (1, 3)), first, diff, gain_ref, shift_ref, [],
        (lat_s, x_s, sems), lambda: None,
    )
    keys_values(x_s, w_ref, kgain_ref, kt_s, v_s)

    def use(p, even, odd):
        sum_ref[2 * p] = even + acc_ref[2 * p]
        sum_ref[2 * p + 1] = odd + acc_ref[2 * p + 1]

    attend(q_ref, kt_s, v_s, use, 8)


def last_kernel(
    own, l0, first, diff, gain_ref, shift_ref, w_ref, kgain_ref, wo_ref, q_ref, acc_ref, out_ref,
    lat_s, x_s, sems, kt_s, v_s, own_s, att_s, own_sem,
):
    rest = [pltpu.make_async_copy(own, own_s, own_sem)]
    prepare(
        (l0,), ((1, 2),), first, diff, gain_ref, shift_ref, rest, (lat_s, x_s, sems), lambda: None
    )
    keys_values(x_s, w_ref, kgain_ref, kt_s, v_s)
    for copy in rest:
        copy.wait()
    lane = lax.broadcasted_iota(jnp.int32, (ROWS, 128), 1) < HEAD

    def use(p, even, odd):
        even = even + acc_ref[2 * p]
        odd = odd + acc_ref[2 * p + 1]
        total = pltpu.roll(jnp.where(lane, odd, even), HEAD, 1)
        f = pl.multiple_of(p * 128, 128)
        att_s[:, pl.ds(f, 128)] = (jnp.where(lane, even, odd) / total).astype(BF16)

    attend(q_ref, kt_s, v_s, use, 8)

    def block(i, carry):
        f = pl.multiple_of(i * 256, 256)
        o = dot(att_s[...], wo_ref[:, pl.ds(f, 256)])
        for k in range(2):
            r = slice(k * TOKF, (k + 1) * TOKF)
            resid = own_s[r, pl.ds(f, 256)].astype(F32) + (
                first[:, pl.ds(f, 256)] + ramp_of(0, 0, k) * diff[:, pl.ds(f, 256)]
            )
            out_ref[r, pl.ds(f, 256)] = (resid + o[r]).astype(BF16)
        return carry

    lax.fori_loop(0, D // 256, block, 0)


def pick_kernel(pair_ref, other_ref, x0, x1, x2, x3, *out_refs):
    zl, x, core = lax.axis_index("zl"), lax.axis_index("x"), lax.axis_index("core")
    for wants, out_ref in zip((pair_ref, other_ref), out_refs):
        for k in range(2):
            wanted = wants[0, k]
            back = (x + X - wanted // CORE % X) % X
            entry = (zl + ZL - wanted // (X * CORE)) % ZL
            back = jnp.where(wanted % CORE == core, back, -1)

            @pl.when(back < 0)
            def _():
                out_ref[k] = jnp.zeros_like(out_ref[k])

            for t, held in enumerate((x0, x1, x2, x3)):

                @pl.when(back == t)
                def _():
                    out_ref[k] = held[entry]


VMEM = pl.BlockSpec(memory_space=pltpu.VMEM)
LIMIT = 32 * 1024 * 1024
SMEM = pl.BlockSpec(memory_space=pltpu.SMEM)
HBM = pl.BlockSpec(memory_space=pltpu.HBM)


def scratch(chunks):
    rows = chunks * ROWS
    return [
        pltpu.VMEM((rows, D), BF16),
        pltpu.VMEM((rows, D), BF16),
        pltpu.SemaphoreType.DMA((chunks,)),
        pltpu.VMEM((D, rows), BF16),
        pltpu.VMEM((rows, D), BF16),
    ]


def body(
    latents, keyframes, key_index, timesteps, mod_weight, norm_gain, qkv_weight, query_gain,
    key_gain, out_weight,
):
    own = latents.reshape(ROWS, D)
    mine = keyframes[0]
    pair = key_index

    near_1, near_3 = send(own, y=1), send(own, y=3)
    pair_other = send(key_index, core=1)
    planes = jnp.stack([after(mine, pair_other), send(mine, zh=1)])
    from_zl = [send(planes, zl=k) for k in (1, 2, 3)]
    by_zl = jnp.stack([planes] + from_zl)
    by_x = [by_zl] + [send(by_zl, x=k) for k in (1, 2, 3)]
    cross = send(after(own, from_zl), zh=1)
    near_2 = send(after(own, (near_1, near_3)), y=2)
    picked = jax.ShapeDtypeStruct((2, ZH, PIECE, D), BF16)
    held, asked = pl.pallas_call(
        pick_kernel,
        out_shape=(picked, picked),
        in_specs=[SMEM] * 2 + [VMEM] * 4,
        out_specs=(VMEM, VMEM),
        name="pick",
    )(key_index, after(pair_other, (near_1, near_3)), *by_x)
    both = after(held, near_2) + send(asked, core=1)
    pieces = [both] + [send(both, y=k) for k in (1, 2, 3)]
    far_1, far_3 = [send(after(cross, both), y=k) for k in (1, 3)]

    halfway = TEMB // 2
    freqs = jnp.exp(-math.log(10000.0) * jnp.arange(halfway, dtype=F32) / halfway)
    angles = timesteps[1].astype(F32) * freqs
    embed = jnp.concatenate([jnp.sin(angles), jnp.cos(angles)]).astype(BF16)[None, :]
    gain, shift, qgain, kgain = pl.pallas_call(
        prelude_kernel,
        out_shape=(jax.ShapeDtypeStruct((1, D), F32),) * 2 + (jax.ShapeDtypeStruct((HEAD, 1), F32),) * 2,
        in_specs=[VMEM] * 7,
        out_specs=(VMEM,) * 4,
        compiler_params=pltpu.CompilerParams(vmem_limit_bytes=LIMIT),
        name="prelude",
    )(
        embed, mod_weight, norm_gain[None, :], query_gain[None, :], key_gain[None, :], qkv_weight,
        out_weight,
    )

    params = pltpu.CompilerParams(vmem_limit_bytes=LIMIT)
    cost = pl.CostEstimate(flops=4 << 30, bytes_accessed=8 << 20, transcendentals=3 << 20)
    sums = jax.ShapeDtypeStruct((HEADS, ROWS, 128), F32)
    token = jax.ShapeDtypeStruct((ROWS, D), BF16)
    table = jax.ShapeDtypeStruct((TOKF, D), F32)
    acc, q, first, diff = pl.pallas_call(
        first_kernel,
        out_shape=(sums, token, table, table),
        in_specs=[SMEM] + [HBM] * 7 + [VMEM] * 5,
        out_specs=(VMEM,) * 4,
        scratch_shapes=scratch(3) + [
            pltpu.VMEM((Y, 2, ZH, PIECE, D), BF16),
            pltpu.SemaphoreType.DMA((Y,)),
        ],
        compiler_params=params,
        cost_estimate=cost,
        name="first_keys",
    )(timesteps, own, near_1, near_3, *pieces, gain, shift, qkv_weight, qgain, kgain)
    far_2 = send(after(cross, acc), y=2)
    acc = pl.pallas_call(
        middle_kernel,
        out_shape=sums,
        in_specs=[HBM] * 4 + [VMEM] * 8,
        out_specs=VMEM,
        scratch_shapes=scratch(4),
        compiler_params=params,
        cost_estimate=cost,
        name="middle_keys",
    )(
        near_2, cross, far_1, far_3, first, diff, gain, shift, qkv_weight, kgain, q, acc,
    )
    out = pl.pallas_call(
        last_kernel,
        out_shape=token,
        in_specs=[HBM] * 2 + [VMEM] * 9,
        out_specs=VMEM,
        scratch_shapes=scratch(1) + [
            pltpu.VMEM((ROWS, D), BF16),
            pltpu.VMEM((ROWS, D), BF16),
            pltpu.SemaphoreType.DMA,
        ],
        compiler_params=params,
        cost_estimate=cost,
        name="last_keys",
    )(
        own, far_2, first, diff, gain, shift, qkv_weight, kgain, out_weight, q, acc,
    )
    return out.reshape(latents.shape)


def solution(mesh):
    split = Mesh(mesh.devices.reshape(ZL, X, CORE, ZH, Y), AXES)
    leaf, seq = ("zl", "x", "core"), ("zh", "y")
    in_specs = (P(leaf, seq, None, None), P(leaf, seq, None), P(leaf, None)) + (P(),) * 7
    out_specs = P(leaf, seq, None, None)
    return jax.shard_map(body, mesh=split, in_specs=in_specs, out_specs=out_specs, check_vma=False)
```

```python
import math

import jax
import jax.numpy as jnp
from jax import lax
from jax.experimental import pallas as pl
from jax.experimental.pallas import tpu as pltpu
from jax.sharding import Mesh
from jax.sharding import PartitionSpec as P

HEADS = 16
HEAD = 64
TEMB = 256
TSTEPS = 1000
D = 1024
FRAMES = 16
TOKF = 128
AXES = ("zl", "x", "core", "zh", "y")
ZL, X, CORE, ZH, Y = 4, 4, 2, 2, 4
ROWS = 256
PIECE = 16
PAIRS = HEADS // 2
F32 = jnp.float32
BF16 = jnp.bfloat16
QSCALE = HEAD ** (-0.5) * math.log2(math.e)


def moves(zl=0, x=0, core=0, zh=0, y=0):
    pairs = []
    for i in range(ZL * X * CORE * ZH * Y):
        rest, iy = divmod(i, Y)
        rest, izh = divmod(rest, ZH)
        rest, ic = divmod(rest, CORE)
        izl, ix = divmod(rest, X)
        izl, ix, ic = (izl + zl) % ZL, (ix + x) % X, (ic + core) % CORE
        izh, iy = (izh + zh) % ZH, (iy + y) % Y
        pairs.append((i, (((izl * X + ix) * CORE + ic) * ZH + izh) * Y + iy))
    return pairs


def send(value, **step):
    return lax.ppermute(value, AXES, moves(**step))


def after(value, earlier):
    return lax.optimization_barrier((value, earlier))[0]


def dot(a, b):
    return jnp.dot(a, b, preferred_element_type=F32)


def dot_tt(a, b):
    return lax.dot_general(a, b, (((0,), (1,)), ((), ())), preferred_element_type=F32)


def blend_tables(time_ref, pieces, first_s, diff_s):
    zh, y = lax.axis_index("zh"), lax.axis_index("y")
    kw = 1.0 - time_ref[0].astype(F32) * (1.0 / (2.0 * TSTEPS))
    for i, piece in enumerate(pieces):
        for z in range(ZH):
            slot = ((zh + z) % ZH) * Y + (y + Y - i) % Y
            base = pl.multiple_of(slot * PIECE, PIECE)
            first = piece[0, z].astype(F32) * kw
            last = piece[1, z].astype(F32) * kw
            first_s[pl.ds(base, PIECE), :] = first
            diff_s[pl.ds(base, PIECE), :] = last - first


def ramp_of(z, back, which):
    zh, y = lax.axis_index("zh"), lax.axis_index("y")
    frame = 2 * (((zh + z) % ZH) * Y + (y + Y - back) % Y) + which
    return frame.astype(F32) * (1.0 / (FRAMES - 1))


def norm_rows(j, i, step, source, lat_s, x_s, first_s, diff_s, gain_ref, shift_ref):
    rows = pl.ds(pl.multiple_of(j * ROWS + i * step, step), step)
    tok = pl.ds(pl.multiple_of(lax.rem(i, TOKF // step) * step, step), step)
    ramp = ramp_of(*source, i // (TOKF // step))
    resid = lat_s[rows, :].astype(F32) + (first_s[tok, :] + ramp * diff_s[tok, :])
    mean = jnp.mean(resid, axis=-1, keepdims=True)
    cent = resid - mean
    var = jnp.mean(cent * cent, axis=-1, keepdims=True)
    normed = cent * lax.rsqrt(var + 1e-06) * gain_ref[...] + shift_ref[...]
    x_s[rows, :] = normed.astype(BF16)


def norm_chunk(j, source, *refs):
    step = 32

    def rows(i, carry):
        norm_rows(j, i, step, source, *refs)
        return carry

    lax.fori_loop(0, ROWS // step, rows, 0, unroll=8)


def head_norm_t(block, gain):
    heads = block.reshape(block.shape[0] // HEAD, HEAD, block.shape[1])
    mean = jnp.mean(heads * heads, axis=1, keepdims=True)
    return (heads * lax.rsqrt(mean + 1e-06) * gain[None]).reshape(block.shape)


def keys_values(x_s, w_ref, kgain_ref, kt_s, v_s):
    kt = dot_tt(w_ref[:, D : 2 * D], x_s[...])
    kt_s[...] = head_norm_t(kt, kgain_ref[...]).astype(BF16)
    v_s[...] = dot(x_s[...], w_ref[:, 2 * D :]).astype(BF16)


def attend(q_s, kt_s, v_s, use, unroll):
    lane = lax.broadcasted_iota(jnp.int32, (ROWS, 128), 1) < HEAD
    lane_v = lax.broadcasted_iota(jnp.int32, (kt_s.shape[1], 128), 1) < HEAD
    one = jnp.ones((), BF16)
    zero = jnp.zeros((), BF16)

    def pair(p, carry):
        f = pl.multiple_of(p * 128, 128)
        qp = q_s[:, pl.ds(f, 128)]
        vp = v_s[:, pl.ds(f, 128)]
        kt = kt_s[pl.ds(f, 128), :]
        even = dot(
            jnp.exp2(dot(jnp.where(lane, qp, zero), kt)).astype(BF16), jnp.where(lane_v, vp, one)
        )
        odd = dot(
            jnp.exp2(dot(jnp.where(lane, zero, qp), kt)).astype(BF16), jnp.where(lane_v, one, vp)
        )
        use(p, even, odd)
        return carry

    lax.fori_loop(0, PAIRS, pair, 0, unroll=unroll)


def prepare(lats, sources, first, diff, gain_ref, shift_ref, copies, scr, between):
    lat_s, x_s, sems = scr
    lat_copies = [
        pltpu.make_async_copy(lat, lat_s.at[pl.ds(j * ROWS, ROWS)], sems.at[j])
        for j, lat in enumerate(lats)
    ]
    for copy in copies + lat_copies:
        copy.start()
    between()
    for j, copy in enumerate(lat_copies):
        copy.wait()
        norm_chunk(j, sources[j], lat_s, x_s, first, diff, gain_ref, shift_ref)


def prelude_kernel(embed_ref, mod_ref, norm_ref, qgain_ref, kgain_ref, w_ref, wo_ref, *out_refs):
    gain, shift, qgain, kgain = out_refs
    embed = jnp.broadcast_to(embed_ref[...], (16, TEMB))
    modulation = dot(embed, mod_ref[...])
    gain[...] = norm_ref[...] * (1.0 + modulation[:1, :D])
    shift[...] = modulation[:1, D:]
    qgain[...] = jnp.broadcast_to(qgain_ref[...] * QSCALE, (8, HEAD)).T[:, :1]
    kgain[...] = jnp.broadcast_to(kgain_ref[...], (8, HEAD)).T[:, :1]


def first_kernel(
    time_ref, l0, l1, l2, p0, p1, p2, p3, gain_ref, shift_ref, w_ref, qgain_ref, kgain_ref,
    acc_ref, q_ref, first, diff, lat_s, x_s, sems, kt_s, v_s, piece_s, piece_sems,
):
    copies = [
        pltpu.make_async_copy(piece, piece_s.at[i], piece_sems.at[i])
        for i, piece in enumerate((p0, p1, p2, p3))
    ]

    def between():
        for copy in copies:
            copy.wait()
        blend_tables(time_ref, [piece_s.at[i] for i in range(Y)], first, diff)

    prepare(
        (l0, l1, l2), ((0, 0), (0, 1), (0, 3)), first, diff, gain_ref, shift_ref, copies,
        (lat_s, x_s, sems), between,
    )
    qt = head_norm_t(dot_tt(w_ref[:, :D], x_s[:ROWS, :]), qgain_ref[...])
    q_ref[...] = qt.astype(BF16).T
    keys_values(x_s, w_ref, kgain_ref, kt_s, v_s)

    def use(p, even, odd):
        acc_ref[2 * p] = even
        acc_ref[2 * p + 1] = odd

    attend(q_ref, kt_s, v_s, use, 8)


def middle_kernel(
    l0, l1, l2, l3, first, diff, gain_ref, shift_ref, w_ref, kgain_ref, q_ref, acc_ref, sum_ref,
    lat_s, x_s, sems, kt_s, v_s,
):
    prepare(
        (l0, l1, l2, l3), ((0, 2), (1, 0), (1, 1), (1, 3)), first, diff, gain_ref, shift_ref, [],
        (lat_s, x_s, sems), lambda: None,
    )
    keys_values(x_s, w_ref, kgain_ref, kt_s, v_s)

    def use(p, even, odd):
        sum_ref[2 * p] = even + acc_ref[2 * p]
        sum_ref[2 * p + 1] = odd + acc_ref[2 * p + 1]

    attend(q_ref, kt_s, v_s, use, 8)


def last_kernel(
    own, l0, first, diff, gain_ref, shift_ref, w_ref, kgain_ref, wo_ref, q_ref, acc_ref, out_ref,
    lat_s, x_s, sems, kt_s, v_s, own_s, att_s, own_sem,
):
    rest = [pltpu.make_async_copy(own, own_s, own_sem)]
    prepare(
        (l0,), ((1, 2),), first, diff, gain_ref, shift_ref, rest, (lat_s, x_s, sems), lambda: None
    )
    keys_values(x_s, w_ref, kgain_ref, kt_s, v_s)
    for copy in rest:
        copy.wait()
    lane = lax.broadcasted_iota(jnp.int32, (ROWS, 128), 1) < HEAD

    def use(p, even, odd):
        even = even + acc_ref[2 * p]
        odd = odd + acc_ref[2 * p + 1]
        total = pltpu.roll(jnp.where(lane, odd, even), HEAD, 1)
        f = pl.multiple_of(p * 128, 128)
        att_s[:, pl.ds(f, 128)] = (jnp.where(lane, even, odd) / total).astype(BF16)

    attend(q_ref, kt_s, v_s, use, 8)

    def block(i, carry):
        f = pl.multiple_of(i * 256, 256)
        o = dot(att_s[...], wo_ref[:, pl.ds(f, 256)])
        for k in range(2):
            r = slice(k * TOKF, (k + 1) * TOKF)
            resid = own_s[r, pl.ds(f, 256)].astype(F32) + (
                first[:, pl.ds(f, 256)] + ramp_of(0, 0, k) * diff[:, pl.ds(f, 256)]
            )
            out_ref[r, pl.ds(f, 256)] = (resid + o[r]).astype(BF16)
        return carry

    lax.fori_loop(0, D // 256, block, 0)


def pick_kernel(pair_ref, other_ref, x0, x1, x2, x3, held_ref, asked_ref, sems):
    zl, x, core = lax.axis_index("zl"), lax.axis_index("x"), lax.axis_index("core")
    slots = []
    for i, (wants, out_ref) in enumerate(((pair_ref, held_ref), (other_ref, asked_ref))):
        for k in range(2):
            wanted = wants[0, k]
            back = (x + X - wanted // CORE % X) % X
            entry = (zl + ZL - wanted // (X * CORE)) % ZL
            sem = sems.at[2 * i + k]
            for t, source in enumerate((x0, x1, x2, x3)):

                @pl.when(back == t)
                def _():
                    pltpu.make_async_copy(source.at[entry], out_ref.at[k], sem).start()

            slots.append((out_ref, k, sem, wanted % CORE == core))
    for out_ref, k, sem, here in slots:
        pltpu.make_async_copy(x0.at[0], out_ref.at[k], sem).wait()

        @pl.when(jnp.logical_not(here))
        def _():
            out_ref[k] = jnp.zeros_like(out_ref[k])


VMEM = pl.BlockSpec(memory_space=pltpu.VMEM)
LIMIT = 32 * 1024 * 1024
SMEM = pl.BlockSpec(memory_space=pltpu.SMEM)
HBM = pl.BlockSpec(memory_space=pltpu.HBM)


def scratch(chunks):
    rows = chunks * ROWS
    return [
        pltpu.VMEM((rows, D), BF16),
        pltpu.VMEM((rows, D), BF16),
        pltpu.SemaphoreType.DMA((chunks,)),
        pltpu.VMEM((D, rows), BF16),
        pltpu.VMEM((rows, D), BF16),
    ]


def body(
    latents, keyframes, key_index, timesteps, mod_weight, norm_gain, qkv_weight, query_gain,
    key_gain, out_weight,
):
    own = latents.reshape(ROWS, D)
    mine = keyframes[0]
    pair = key_index

    near_1, near_3 = send(own, y=1), send(own, y=3)
    pair_other = send(key_index, core=1)
    planes = jnp.stack([after(mine, pair_other), send(mine, zh=1)])
    from_zl = [send(planes, zl=k) for k in (1, 2, 3)]
    by_zl = jnp.stack([planes] + from_zl)
    by_x = [by_zl] + [send(by_zl, x=k) for k in (1, 2, 3)]
    cross = send(after(own, from_zl), zh=1)
    near_2 = send(after(own, (near_1, near_3)), y=2)
    picked = jax.ShapeDtypeStruct((2, ZH, PIECE, D), BF16)
    held, asked = pl.pallas_call(
        pick_kernel,
        out_shape=(picked, picked),
        in_specs=[SMEM] * 2 + [HBM] * 4,
        out_specs=(VMEM, VMEM),
        scratch_shapes=[pltpu.SemaphoreType.DMA((4,))],
        name="pick",
    )(key_index, after(pair_other, (near_1, near_3)), *by_x)
    both = after(held, near_2) + send(asked, core=1)
    pieces = [both] + [send(both, y=k) for k in (1, 2, 3)]
    far_1, far_3 = [send(after(cross, both), y=k) for k in (1, 3)]

    halfway = TEMB // 2
    freqs = jnp.exp(-math.log(10000.0) * jnp.arange(halfway, dtype=F32) / halfway)
    angles = timesteps[1].astype(F32) * freqs
    embed = jnp.concatenate([jnp.sin(angles), jnp.cos(angles)]).astype(BF16)[None, :]
    gain, shift, qgain, kgain = pl.pallas_call(
        prelude_kernel,
        out_shape=(jax.ShapeDtypeStruct((1, D), F32),) * 2 + (jax.ShapeDtypeStruct((HEAD, 1), F32),) * 2,
        in_specs=[VMEM] * 7,
        out_specs=(VMEM,) * 4,
        compiler_params=pltpu.CompilerParams(vmem_limit_bytes=LIMIT),
        name="prelude",
    )(
        embed, mod_weight, norm_gain[None, :], query_gain[None, :], key_gain[None, :], qkv_weight,
        out_weight,
    )

    params = pltpu.CompilerParams(vmem_limit_bytes=LIMIT)
    cost = pl.CostEstimate(flops=4 << 30, bytes_accessed=8 << 20, transcendentals=3 << 20)
    sums = jax.ShapeDtypeStruct((HEADS, ROWS, 128), F32)
    token = jax.ShapeDtypeStruct((ROWS, D), BF16)
    table = jax.ShapeDtypeStruct((TOKF, D), F32)
    acc, q, first, diff = pl.pallas_call(
        first_kernel,
        out_shape=(sums, token, table, table),
        in_specs=[SMEM] + [HBM] * 7 + [VMEM] * 5,
        out_specs=(VMEM,) * 4,
        scratch_shapes=scratch(3) + [
            pltpu.VMEM((Y, 2, ZH, PIECE, D), BF16),
            pltpu.SemaphoreType.DMA((Y,)),
        ],
        compiler_params=params,
        cost_estimate=cost,
        name="first_keys",
    )(timesteps, own, near_1, near_3, *pieces, gain, shift, qkv_weight, qgain, kgain)
    far_2 = send(after(cross, acc), y=2)
    acc = pl.pallas_call(
        middle_kernel,
        out_shape=sums,
        in_specs=[HBM] * 4 + [VMEM] * 8,
        out_specs=VMEM,
        scratch_shapes=scratch(4),
        compiler_params=params,
        cost_estimate=cost,
        name="middle_keys",
    )(
        near_2, cross, far_1, far_3, first, diff, gain, shift, qkv_weight, kgain, q, acc,
    )
    out = pl.pallas_call(
        last_kernel,
        out_shape=token,
        in_specs=[HBM] * 2 + [VMEM] * 9,
        out_specs=VMEM,
        scratch_shapes=scratch(1) + [
            pltpu.VMEM((ROWS, D), BF16),
            pltpu.VMEM((ROWS, D), BF16),
            pltpu.SemaphoreType.DMA,
        ],
        compiler_params=params,
        cost_estimate=cost,
        name="last_keys",
    )(
        own, far_2, first, diff, gain, shift, qkv_weight, kgain, out_weight, q, acc,
    )
    return out.reshape(latents.shape)


def solution(mesh):
    split = Mesh(mesh.devices.reshape(ZL, X, CORE, ZH, Y), AXES)
    leaf, seq = ("zl", "x", "core"), ("zh", "y")
    in_specs = (P(leaf, seq, None, None), P(leaf, seq, None), P(leaf, None)) + (P(),) * 7
    out_specs = P(leaf, seq, None, None)
    return jax.shard_map(body, mesh=split, in_specs=in_specs, out_specs=out_specs, check_vma=False)
```
